256 devices in a mesh: ctx: 32 (over x, z_lo, y), state: 8 (over z_hi, core).
Axes of the slice: x: 4, y: 4, z: 8 (z_hi: 4, z_lo: 2; z = z_hi * 2 + z_lo), core: 2. Of those that a mesh axis runs over, the one named last changes fastest.
Arguments:
- key_rows: bfloat16 [12288, 1024], P('ctx'), may hold values from -12 to 12
- value_rows: bfloat16 [12288, 1024], P('ctx'), may hold values from -12 to 12
- token_rates: float32 [12288], P('ctx'), may hold values from 0.1 to 1
- query_rows: bfloat16 [12288, 1024], P('ctx'), may hold values from -6 to 6
- fast_gate: bfloat16 [1024, 12288], P('ctx', 'state'), may hold values from -0.1875 to 0.1875
- fast_up: bfloat16 [1024, 12288], P('ctx', 'state'), may hold values from -0.1875 to 0.1875
- fast_down: bfloat16 [12288, 1024], P('state', 'ctx'), may hold values from -0.0546875 to 0.0546875
Outputs:
- next_out: bfloat16 [12288, 1024], P('ctx', 'state')
The draws below stay inside these ranges and needn't reach their ends.
All inputs are finite; a program needn't handle non-finite values.
Results may differ from the reference program's by a relative error of at most 0.025.
Values may be sent and summed in bfloat16 or wider, within the bound.
A program may use at most 128 MiB of HBM per device.

```python
import math
import jax
import jax.numpy as jnp
from jax import lax

DK = 1024
FH = 12288
TOK_DEV = 384
TOKENS = 12288
N_CTX = 32


def column_scaled(key, low_scale, ratio):
    column_key, entry_key = jax.random.split(key)
    position = jnp.mod(2 * jnp.arange(DK, dtype=jnp.int32), DK).astype(jnp.float32) / DK
    jitter = jax.random.uniform(column_key, (DK,), jnp.float32, 0.7, 1.3)
    column_scale = low_scale * jnp.power(ratio, position) * jitter
    entries = jax.random.normal(entry_key, (TOKENS, DK), jnp.float32)
    return jnp.clip(entries * column_scale[None, :], -12.0, 12.0)


def draw_key_rows(key, part):
    key = jax.random.fold_in(key, 11)
    values = column_scaled(key, 0.3, 10.0)
    return values.astype(jnp.bfloat16)


def draw_value_rows(key, part):
    key = jax.random.fold_in(key, 23)
    values = column_scaled(key, 0.3, 10.0)
    return values.astype(jnp.bfloat16)


def levels(key, dims, shards, smallest, high):
    factor_of, own = 1.0, jax.random.fold_in(key, 6)
    for axis_at, blocks in shards:
        draws = jnp.exp(jax.random.uniform(jax.random.fold_in(own, axis_at), (blocks,), jnp.float32, smallest / len(shards), high / len(shards)))
        factor_of = factor_of * jnp.repeat(draws, dims[axis_at] // blocks).reshape([-1 if axis == axis_at else 1 for axis in range(len(dims))])
    return factor_of


def scatter_about(own_key, extent, scale, reach, shards=(), held_as=jnp.bfloat16):
    result = scale * jax.random.normal(own_key, extent, jnp.float32)
    if shards:
        result = result * levels(own_key, extent, shards, -0.22, 0.18)
    return jnp.clip(result, -reach, reach).astype(held_as)


def setup_inputs(seed: int = 0) -> dict:
    seeds = jax.random.split(jax.random.key(seed), 8)
    key_rows = draw_key_rows(jax.random.fold_in(seeds[7], 71), 0)
    value_rows = draw_value_rows(jax.random.fold_in(seeds[7], 71), 0)
    token_rates = jnp.clip(jnp.exp(math.log(1.0) - 2.3025851 * jax.random.uniform(seeds[2], (TOKENS,), jnp.float32) ** levels(seeds[2], (TOKENS,), ((0, 32),), -0.2, 0.2)), 0.1, 1.0)
    query_rows = scatter_about(seeds[3], (TOKENS, DK), 1.0, 6.0, ((0, 32),))
    fast_gate = scatter_about(seeds[4], (DK, FH), DK ** -0.5, 0.1875, ((0, 32), (1, 8)))
    fast_up = scatter_about(seeds[5], (DK, FH), DK ** -0.5, 0.1875, ((0, 32), (1, 8)))
    fast_down = scatter_about(seeds[6], (FH, DK), FH ** -0.5, 0.0546875, ((0, 8), (1, 32)))
    return {"key_rows": key_rows, "value_rows": value_rows, "token_rates": token_rates, "query_rows": query_rows, "fast_gate": fast_gate, "fast_up": fast_up, "fast_down": fast_down}


epsilon = 1e-06
step_rate = 0.5

def swiglu_parts(gate_pre):
    sigmoid_gate = jax.nn.sigmoid(gate_pre)
    return (gate_pre * sigmoid_gate, sigmoid_gate)

def renew(weight_units, direction):
    weight_float = weight_units.astype(jnp.float32)
    weight_sq = lax.optimization_barrier(jnp.sum(weight_float * weight_float, axis=-1, keepdims=True))
    direction_sq = lax.optimization_barrier(jnp.sum(direction * direction, axis=-1, keepdims=True))
    weight_norm = jnp.sqrt(weight_sq + epsilon)
    stepped = weight_float + step_rate * weight_norm / jnp.sqrt(direction_sq + epsilon) * direction
    stepped_sq = lax.optimization_barrier(jnp.sum(stepped * stepped, axis=-1, keepdims=True))
    return (stepped * (weight_norm / jnp.sqrt(stepped_sq + epsilon))).astype(jnp.bfloat16)

def reference(key_rows, value_rows, token_rates, query_rows, fast_gate, fast_up, fast_down):
    key_blocks = key_rows.reshape(N_CTX, TOK_DEV, DK)
    value_blocks = value_rows.reshape(N_CTX, TOK_DEV, DK)
    rate_blocks = token_rates.reshape(N_CTX, TOK_DEV)

    def accumulate(running, pieces):
        key_block, value_block, rate_block = pieces
        gate_pre = jnp.dot(key_block, fast_gate, preferred_element_type=jnp.float32)
        up_pre = jnp.dot(key_block, fast_up, preferred_element_type=jnp.float32)
        silu_gate, sigmoid_gate = swiglu_parts(gate_pre)
        hidden = (silu_gate * up_pre).astype(jnp.bfloat16)
        target = (value_block.astype(jnp.float32) * rate_block[:, None]).astype(jnp.bfloat16)
        back_grad = jnp.dot(target, fast_down.T, preferred_element_type=jnp.float32)
        grad_gate = (back_grad * up_pre * sigmoid_gate * (1.0 + gate_pre * (1.0 - sigmoid_gate))).astype(jnp.bfloat16)
        grad_up = (back_grad * silu_gate).astype(jnp.bfloat16)
        partials = (jnp.dot(grad_gate.T, key_block, preferred_element_type=jnp.float32), jnp.dot(grad_up.T, key_block, preferred_element_type=jnp.float32), jnp.dot(hidden.T, target, preferred_element_type=jnp.float32))
        rounded = lax.optimization_barrier(tuple((member.astype(jnp.bfloat16) for member in partials)))
        return (tuple((prior + member.astype(jnp.float32) for prior, member in zip(running, rounded))), None)
    zeros_init = jnp.zeros((FH, DK), jnp.float32)
    directions, unused = lax.scan(accumulate, (zeros_init, zeros_init, zeros_init), (key_blocks, value_blocks, rate_blocks))
    new_gate = renew(fast_gate.T, directions[0])
    new_up = renew(fast_up.T, directions[1])
    new_down = renew(fast_down, directions[2])

    def apply_block(query_block):
        gate_next = jnp.dot(query_block, new_gate.T, preferred_element_type=jnp.float32)
        up_next = jnp.dot(query_block, new_up.T, preferred_element_type=jnp.float32)
        silu_next, sigmoid_next = swiglu_parts(gate_next)
        hidden_next = (silu_next * up_next).astype(jnp.bfloat16)
        return jnp.dot(hidden_next, new_down, preferred_element_type=jnp.float32).astype(jnp.bfloat16)
    outputs = lax.map(apply_block, query_rows.reshape(N_CTX, TOK_DEV, DK))
    return outputs.reshape(N_CTX * TOK_DEV, DK)
```

```python
import functools

import jax
import jax.numpy as jnp
from jax import lax
from jax.experimental import pallas as pl
from jax.experimental.pallas import tpu as pltpu
from jax.sharding import PartitionSpec as P

MESH = pl.DeviceIdType.MESH
EPS = 1e-06
RATE = 0.5
NT = (((1,), (1,)), ((), ()))
NN = (((1,), (0,)), ((), ()))
F32, BF16 = jnp.float32, jnp.bfloat16
N_SEM = 160


def dot(a, b, dims):
    return lax.dot_general(a, b, dims, preferred_element_type=F32)


def place(x, y, z, k):
    return (x * 8 + (z % 2) * 4 + y, (z // 2) * 2 + k)


class Links:
    def __init__(self, send_sem, recv_sem):
        self.send_sem, self.recv_sem, self.used, self.sent = send_sem, recv_sem, 0, []

    def ids(self, count=1):
        first = self.used
        self.used += count
        assert self.used <= N_SEM
        return first

    def send(self, index, src, dst, device):
        copy = pltpu.make_async_remote_copy(
            src_ref=src, dst_ref=dst, send_sem=self.send_sem.at[index], recv_sem=self.recv_sem.at[index],
            device_id=device, device_id_type=MESH)
        copy.start()
        self.sent.append(copy)

    def wait(self, index, dst, device):
        pltpu.make_async_remote_copy(
            src_ref=dst, dst_ref=dst, send_sem=self.send_sem.at[index], recv_sem=self.recv_sem.at[index],
            device_id=device, device_id_type=MESH).wait_recv()

    def drain(self):
        for copy in self.sent:
            copy.wait_send()


def kernel(key_ref, val_ref, rate_ref, qry_ref, gate_ref, up_ref, down_ref, out_ref,
           key_all, val_all, qry_all, rates, quarter, w, gp, uq, hid, grads,
           d, ry0, x1a0, x1b0, x2a0, x2b0, x1a, x1b, x2a, x2b, e, es, ry, new,
           ob, osib, r, ryo, za0, zb0, za, zb, ya0, yb0, ya, ybuf, fin, fins, yfin,
           send_sem, recv_sem, local_sem):
    c, s = lax.axis_index("ctx"), lax.axis_index("state")
    x, zlo, y = c // 8, (c // 4) % 2, c % 4
    zhi, k = s // 2, s % 2
    z = 2 * zhi + zlo
    p, yb = y // 2, y % 2
    xp, xm, xo = (x + 1) % 4, (x + 3) % 4, (x + 2) % 4
    zp, zm = (z + 1) % 8, (z + 7) % 8
    yt = y + 1 - 2 * yb
    yr = 3 - y
    po = 1 - p
    links = Links(send_sem, recv_sem)
    dev_xp, dev_xm = place(xp, y, z, k), place(xm, y, z, k)
    dev_yt, dev_yr = place(x, yt, z, k), place(x, yr, z, k)
    dev_zp, dev_zm = place(x, y, zp, k), place(x, y, zm, k)
    dev_core = place(x, y, z, 1 - k)
    z_pair = z + 1 - 2 * zlo
    z_other = jnp.where(zlo == 0, zm, zp)

    def block(yy, zz):
        return 2 * yy + zz

    me = block(yb, zlo)

    full = [key_all, val_all, qry_all]
    src = [key_ref, val_ref, qry_ref]
    local = []
    for i in range(3):
        copy = pltpu.make_async_copy(
            src[i], full[i].at[pl.ds(pl.multiple_of(me * 384, 16), 384)], local_sem.at[i])
        copy.start()
        local.append(copy)

    barrier = pltpu.get_barrier_semaphore()
    for dy in range(4):
        for dz in range(2):
            if dy or dz:
                pl.semaphore_signal(barrier, inc=1, device_id=place(x, (y + dy) % 4, 2 * zhi + (zlo + dz) % 2, k), device_id_type=MESH)
    for other in (dev_xp, dev_xm, place(x, y, z_other, k), dev_core):
        pl.semaphore_signal(barrier, inc=1, device_id=other, device_id_type=MESH)
    pl.semaphore_wait(barrier, 11)

    first = links.ids(12)
    weights = [gate_ref, up_ref, down_ref]
    stage = []
    for a in range(3):
        for qz in range(2):
            for q2 in range(2):
                ty = jnp.where(zlo == 0, q2, 3 - q2)
                own = jnp.logical_and(ty == y, zlo == qz)
                piece = weights[a].at[:, pl.ds((qz * 2 + q2) * 384, 384)]
                into = quarter.at[a, pl.ds(pl.multiple_of(32 * y, 32), 32)]
                copy = pltpu.make_async_remote_copy(
                    src_ref=piece, dst_ref=into, send_sem=send_sem.at[first + a * 4 + qz * 2 + q2],
                    recv_sem=recv_sem.at[first + a * 4 + y],
                    device_id=place(x, ty, 2 * zhi + qz, k), device_id_type=MESH)
                stay = pltpu.make_async_copy(piece, into, local_sem.at[3 + a])
                stage.append((own, copy, stay))

                @pl.when(own)
                def _():
                    stay.start()

                @pl.when(jnp.logical_not(own))
                def _():
                    copy.start()

    rate_id = links.ids(3)

    def rate_at(b):
        return rates.at[:, pl.ds(pl.multiple_of(b * 384, 128), 384)]

    rate_copy = pltpu.make_async_copy(rate_ref, rate_at(me), local_sem.at[6])
    rate_copy.start()
    links.send(rate_id, rate_ref, rate_at(me), dev_yt)
    links.send(rate_id + 1, rate_ref, rate_at(me), place(x, y, z_pair, k))
    links.send(rate_id + 2, rate_ref, rate_at(me), place(x, yt, z_pair, k))

    blocks = {"a": block(1 - yb, zlo), "b": block(yb, 1 - zlo), "c": block(1 - yb, 1 - zlo)}
    tok_ids = {(i, kind, h): links.ids() for i in range(3) for kind in "abc" for h in range(2)}
    sib_ids = {(i, kind, h): links.ids() for i in range(3) for kind in "abc" for h in range(2)}

    def rows(i, b, h, kk=k):
        return full[i].at[pl.ds(pl.multiple_of(b * 384 + kk * 192 + h * 96, 16), 96)]

    z_to = [dev_zp, dev_zm]

    def token_start(i):
        for h in range(2):
            mine = src[i].at[pl.ds(pl.multiple_of(k * 192 + h * 96, 16), 96)]
            links.send(tok_ids[i, "a", h], mine, rows(i, me, h), dev_yt)
            links.send(tok_ids[i, "b", h], mine, rows(i, me, h), z_to[h])

    def token_pass(i, kind):
        for h in range(2):
            here = rows(i, blocks[kind], h)
            links.wait(tok_ids[i, kind, h], here, dev_core)
            if kind == "a":
                links.send(tok_ids[i, "c", h], here, here, z_to[h])
            links.send(sib_ids[i, kind, h], here, here, dev_core)

    def token_finish(i):
        for kind in "abc":
            for h in range(2):
                links.wait(sib_ids[i, kind, h], rows(i, blocks[kind], h, 1 - k), dev_core)

    def gather(piece, half):
        base = {name: links.ids(3) for name in ("xp", "xm", "y", "fp", "fm", "xp2", "xm2", "fp2", "fm2", "y1", "y2", "y3")}

        def start(a):
            links.send(base["xp"] + a, piece(a, x, p), piece(a, x, p), dev_xp)
            links.send(base["xm"] + a, piece(a, x, p), piece(a, x, p), dev_xm)
            links.send(base["y"] + a, piece(a, x, p), piece(a, x, p), dev_yr)

        def cross(a):
            links.wait(base["y"] + a, piece(a, x, po), dev_yr)
            links.send(base["xp2"] + a, piece(a, x, po), piece(a, x, po), dev_xp)
            links.send(base["xm2"] + a, piece(a, x, po), piece(a, x, po), dev_xm)

        def onward(a, which, pp):
            links.wait(base["xp" + which] + a, piece(a, xm, pp), dev_xm)
            links.send(base["fp" + which] + a, half(a, xm, pp, 0), half(a, xm, pp, 0), dev_xp)
            if a == 0:
                links.send(base["y1"], piece(a, xm, pp), piece(a, xm, pp), dev_yr)
            links.wait(base["xm" + which] + a, piece(a, xp, pp), dev_xp)
            links.send(base["fm" + which] + a, half(a, xp, pp, 1), half(a, xp, pp, 1), dev_xm)
            if a == 0:
                links.send(base["y2"], piece(a, xp, pp), piece(a, xp, pp), dev_yr)

        def far(a, which, pp):
            links.wait(base["fp" + which] + a, half(a, xo, pp, 0), dev_xm)
            links.wait(base["fm" + which] + a, half(a, xo, pp, 1), dev_xp)
            if a == 0:
                links.send(base["y3"], piece(a, xo, pp), piece(a, xo, pp), dev_yr)

        def finish(a):
            if a == 0:
                links.wait(base["y"], piece(a, x, po), dev_yr)
                links.wait(base["y1"], piece(a, xm, po), dev_yr)
                links.wait(base["y2"], piece(a, xp, po), dev_yr)
                links.wait(base["y3"], piece(a, xo, po), dev_yr)
            else:
                far(a, "2", po)

        return start, cross, onward, far, finish

    def w_piece(a, xx, pp):
        return w.at[a, :, pl.ds(pl.multiple_of((2 * xx + pp) * 128, 128), 128)]

    def w_half(a, xx, pp, h):
        return w.at[a, pl.ds(192 * h, 192), pl.ds(pl.multiple_of((2 * xx + pp) * 128, 128), 128)]

    token_start(0)
    w_start, w_cross, w_onward, w_far, w_finish = gather(w_piece, w_half)
    for a in range(3):
        for own, copy, stay in stage[4 * a:4 * a + 4]:
            @pl.when(own)
            def _():
                stay.wait()

        for ys in range(4):
            @pl.when(jnp.logical_or(ys != y, zlo != p))
            def _():
                links.wait(first + a * 4 + ys, quarter.at[a, pl.ds(32 * ys, 32)], dev_core)
        w_piece(a, x, p)[...] = quarter[a].astype(F32).T.astype(BF16)
        w_start(a)
    token_start(1)
    token_pass(0, "b")
    token_pass(0, "a")
    w_cross(1)
    w_cross(2)
    w_onward(0, "", p)
    w_onward(1, "", p)
    token_pass(0, "c")
    token_pass(1, "b")
    token_pass(1, "a")
    w_onward(2, "", p)
    w_far(0, "", p)
    w_onward(1, "2", po)
    w_onward(2, "2", po)
    token_start(2)
    token_pass(1, "c")
    for copy in local:
        copy.wait()
    rate_copy.wait()
    for i, b in enumerate(("a", "b", "c")):
        links.wait(rate_id + i, rate_at(blocks[b]), dev_core)
    token_finish(0)
    w_finish(0)
    w_far(1, "", p)
    w_finish(1)

    def forward(t, carry):
        cols = pl.ds(pl.multiple_of(t * 512, 512), 512)
        keys = key_all[cols, :]
        gate_pre = dot(w[0], keys, NT)
        up_pre = dot(w[1], keys, NT)
        gp[:, cols] = gate_pre
        uq[:, cols] = up_pre
        hid[:, cols] = (gate_pre * jax.nn.sigmoid(gate_pre) * up_pre * rates[:, cols]).astype(BF16)
        return carry

    lax.fori_loop(0, 3, forward, 0)
    token_finish(1)

    def direction(a, acts, tokens):
        def part(n, carry):
            cols = pl.ds(pl.multiple_of(n * 256, 256), 256)
            term = dot(acts[...], tokens[:, cols], NN)
            d[a, :, :, :, cols] = term.reshape(4, 2, 48, 256).astype(BF16)
            return carry
        lax.fori_loop(0, 4, part, 0)

    rs = {name: links.ids(3) for name in ("ap", "bm", "p", "m", "y")}
    ab = [pl.ds(0, 512), pl.ds(512, 512)]

    def reduce_start(a):
        links.send(rs["ap"] + a, d.at[a, xo, :, :, ab[0]], x1a.at[a - 1], dev_xp)
        links.send(rs["bm"] + a, d.at[a, xo, :, :, ab[1]], x1b.at[a - 1], dev_xm)

    def reduce_merge(a):
        links.wait(rs["ap"] + a, x1a.at[a - 1], dev_xm)
        d[a, xp, :, :, ab[0]] = (d[a, xp, :, :, ab[0]].astype(F32) + x1a[a - 1].astype(F32)).astype(BF16)
        links.send(rs["p"] + a, d.at[a, xp], x2a.at[a - 1], dev_xp)
        links.wait(rs["bm"] + a, x1b.at[a - 1], dev_xp)
        d[a, xm, :, :, ab[1]] = (d[a, xm, :, :, ab[1]].astype(F32) + x1b[a - 1].astype(F32)).astype(BF16)
        links.send(rs["m"] + a, d.at[a, xm], x2b.at[a - 1], dev_xm)

    def reduce_cross(a):
        links.wait(rs["p"] + a, x2a.at[a - 1], dev_xm)
        links.wait(rs["m"] + a, x2b.at[a - 1], dev_xp)
        total = d[a, x].astype(F32) + x2a[a - 1].astype(F32) + x2b[a - 1].astype(F32)
        e[a - 1] = total
        es[a - 1] = total.astype(BF16)
        links.send(rs["y"] + a, es.at[a - 1, po], ry.at[a - 1], dev_yr)

    def renew(a, grad):
        unit = pl.ds(pl.multiple_of((2 * x + p) * 48, 16), 48)
        old = w[a, unit, :].astype(F32)
        norm = jnp.sqrt(jnp.sum(old * old, axis=1, keepdims=True) + EPS)
        stepped = old + RATE * norm / jnp.sqrt(jnp.sum(grad * grad, axis=1, keepdims=True) + EPS) * grad
        scale = norm / jnp.sqrt(jnp.sum(stepped * stepped, axis=1, keepdims=True) + EPS)
        new[a, x, p] = (stepped * scale).astype(BF16)

    direction(2, hid, val_all)
    reduce_start(2)
    w_far(2, "", p)
    w_finish(2)

    def backward(t, carry):
        cols = pl.ds(pl.multiple_of(t * 512, 512), 512)
        back = dot(w[2], val_all[cols, :], NT) * rates[:, cols]
        gate_pre, up_pre = gp[:, cols], uq[:, cols]
        sig = jax.nn.sigmoid(gate_pre)
        grads[0, :, cols] = (back * up_pre * sig * (1.0 + gate_pre * (1.0 - sig))).astype(BF16)
        grads[1, :, cols] = (back * gate_pre * sig).astype(BF16)
        return carry

    lax.fori_loop(0, 3, backward, 0)
    direction(0, grads.at[0], key_all)
    links.send(rs["y"], d.at[0, :, po], ry0, dev_yr)
    direction(1, grads.at[1], key_all)
    reduce_start(1)
    reduce_merge(2)
    links.wait(rs["y"], ry0, dev_yr)
    d[0, :, p] = (d[0, :, p].astype(F32) + ry0[...].astype(F32)).astype(BF16)
    links.send(rs["ap"], d.at[0, xo, p, :, ab[0]], x1a0, dev_xp)
    links.send(rs["bm"], d.at[0, xo, p, :, ab[1]], x1b0, dev_xm)
    reduce_merge(1)
    token_pass(2, "b")
    token_pass(2, "a")
    links.wait(rs["ap"], x1a0, dev_xm)
    d[0, xp, p, :, ab[0]] = (d[0, xp, p, :, ab[0]].astype(F32) + x1a0[...].astype(F32)).astype(BF16)
    links.send(rs["p"], d.at[0, xp, p], x2a0, dev_xp)
    links.wait(rs["bm"], x1b0, dev_xp)
    d[0, xm, p, :, ab[1]] = (d[0, xm, p, :, ab[1]].astype(F32) + x1b0[...].astype(F32)).astype(BF16)
    links.send(rs["m"], d.at[0, xm, p], x2b0, dev_xm)
    reduce_cross(2)
    reduce_cross(1)
    token_pass(2, "c")

    def n_piece(a, xx, pp):
        return new.at[a, xx, pp]

    def n_half(a, xx, pp, h):
        return new.at[a, xx, pp, :, ab[h]]

    n_start, n_cross, n_onward, n_far, n_finish = gather(n_piece, n_half)
    links.wait(rs["p"], x2a0, dev_xm)
    links.wait(rs["m"], x2b0, dev_xp)
    renew(0, d[0, x, p].astype(F32) + x2a0[...].astype(F32) + x2b0[...].astype(F32))
    n_start(0)
    for a in (2, 1):
        links.wait(rs["y"] + a, ry.at[a - 1], dev_yr)
        renew(a, e[a - 1, p] + ry[a - 1].astype(F32))
        n_start(a)
    n_onward(0, "", p)
    n_cross(2)
    n_cross(1)
    n_onward(2, "", p)
    n_onward(1, "", p)
    n_far(0, "", p)
    n_onward(2, "2", po)
    n_onward(1, "2", po)
    n_far(2, "", p)
    n_far(1, "", p)
    token_finish(2)
    n_finish(0)
    n_finish(1)
    n_finish(2)

    core_ids = links.ids(4)

    def apply(b, carry):
        q = qry_all[pl.ds(pl.multiple_of(b * 384, 16), 384), :]
        gate_next = dot(q, new[0].reshape(384, 1024), NT)
        up_next = dot(q, new[1].reshape(384, 1024), NT)
        act = (gate_next * jax.nn.sigmoid(gate_next) * up_next).astype(BF16)
        term = dot(act, new[2].reshape(384, 1024), NN)
        for zz in range(4):
            for kk in range(2):
                at = (2 * zz + kk) * 128
                ob[b, kk, zz] = term[:, at:at + 128].astype(BF16)
        return carry

    for b in range(4):
        apply(b, 0)
        links.send(core_ids + b, ob.at[b, 1 - k], osib.at[b], dev_core)
    for b in range(4):
        links.wait(core_ids + b, osib.at[b], dev_core)
        r[b // 2, b % 2] = (ob[b, k].astype(F32) + osib[b].astype(F32)).astype(BF16)

    lo, hi = pl.ds(0, 192), pl.ds(192, 192)
    y_id = links.ids()
    links.send(y_id, r.at[1 - yb, :, :, lo], ryo, dev_yt)
    ring = {name: links.ids(4) for name in ("zp", "zm", "yp", "ym")}

    def at(step, sign):
        t = (z + sign * (4 - step) + 8) % 8
        return t % 2, t // 2

    def chunk(kind, t, part):
        if kind == "z":
            return (slice(None), t[0], t[1], pl.ds(192 + part[0], part[1]))
        return (yb, t[0], t[1], pl.ds(part[0], part[1]))

    halves = {1: (0, 96), -1: (96, 96)}
    slots = {("z", 1): (za0, za), ("z", -1): (zb0, zb), ("y", 1): (ya0, ya), ("y", -1): (yb0, ybuf)}

    def slot(kind, sign, step):
        return slots[kind, sign][0] if step == 0 else slots[kind, sign][1].at[step - 1]

    def ring_send(kind, sign, step):
        part = halves[sign] if step == 0 else (0, 192)
        links.send(ring[kind + ("p" if sign > 0 else "m")] + step, r.at[chunk(kind, at(step, sign), part)],
                   slot(kind, sign, step), dev_zp if sign > 0 else dev_zm)

    def ring_recv(kind, sign, step):
        got = slot(kind, sign, step)
        links.wait(ring[kind + ("p" if sign > 0 else "m")] + step, got, dev_zm if sign > 0 else dev_zp)
        return got

    def ring_add(kind, sign, step):
        got = ring_recv(kind, sign, step)
        where = chunk(kind, at(step + 1, sign), halves[sign] if step == 0 else (0, 192))
        r[where] = (r[where].astype(F32) + got[...].astype(F32)).astype(BF16)

    for sign in (1, -1):
        ring_send("z", sign, 0)
    links.wait(y_id, ryo, dev_yt)
    r[yb, :, :, lo] = (r[yb, :, :, lo].astype(F32) + ryo[...].astype(F32)).astype(BF16)
    for sign in (1, -1):
        ring_send("y", sign, 0)
    for step in range(1, 4):
        for kind in ("z", "y"):
            for sign in (1, -1):
                ring_add(kind, sign, step - 1)
                ring_send(kind, sign, step)
    got = [ring_recv("z", sign, 3) for sign in (1, -1)]
    total = r[:, zlo, zhi, hi].astype(F32) + got[0][...].astype(F32) + got[1][...].astype(F32)
    fin[...] = total
    fins[...] = total.astype(BF16)
    fin_id = links.ids()
    links.send(fin_id, fins.at[1 - yb], yfin, dev_yt)
    got = [ring_recv("y", sign, 3) for sign in (1, -1)]
    out_ref[lo, :] = (r[yb, zlo, zhi, lo].astype(F32) + got[0][...].astype(F32) + got[1][...].astype(F32)).astype(BF16)
    links.wait(fin_id, yfin, dev_yt)
    out_ref[hi, :] = (fin[yb] + yfin[...].astype(F32)).astype(BF16)

    for own, copy, stay in stage:
        @pl.when(jnp.logical_not(own))
        def _():
            copy.wait_send()
    links.drain()


def on_device(key_rows, value_rows, token_rates, query_rows, fast_gate, fast_up, fast_down):
    any_spec = pl.BlockSpec(memory_space=pl.ANY)
    vmem = pl.BlockSpec(memory_space=pltpu.VMEM)
    V = pltpu.VMEM
    scratch = [
        V((1536, 1024), BF16), V((1536, 1024), BF16), V((1536, 1024), BF16), V((1, 1536), F32),
        V((3, 128, 384), BF16), V((3, 384, 1024), BF16),
        V((384, 1536), F32), V((384, 1536), F32), V((384, 1536), BF16), V((2, 384, 1536), BF16),
        V((3, 4, 2, 48, 1024), BF16),
        V((4, 48, 1024), BF16), V((48, 512), BF16), V((48, 512), BF16), V((48, 1024), BF16), V((48, 1024), BF16),
        V((2, 2, 48, 512), BF16), V((2, 2, 48, 512), BF16), V((2, 2, 48, 1024), BF16), V((2, 2, 48, 1024), BF16),
        V((2, 2, 48, 1024), F32), V((2, 2, 48, 1024), BF16), V((2, 48, 1024), BF16),
        V((3, 4, 2, 48, 1024), BF16),
        V((4, 2, 4, 384, 128), BF16), V((4, 4, 384, 128), BF16), V((2, 2, 4, 384, 128), BF16),
        V((2, 4, 192, 128), BF16),
        V((2, 96, 128), BF16), V((2, 96, 128), BF16), V((3, 2, 192, 128), BF16), V((3, 2, 192, 128), BF16),
        V((96, 128), BF16), V((96, 128), BF16), V((3, 192, 128), BF16), V((3, 192, 128), BF16),
        V((2, 192, 128), F32), V((2, 192, 128), BF16), V((192, 128), BF16),
        pltpu.SemaphoreType.DMA((N_SEM,)), pltpu.SemaphoreType.DMA((N_SEM,)), pltpu.SemaphoreType.DMA((8,)),
    ]
    return pl.pallas_call(
        kernel,
        out_shape=jax.ShapeDtypeStruct((384, 128), BF16),
        in_specs=[any_spec, any_spec, any_spec, any_spec, any_spec, any_spec, any_spec],
        out_specs=vmem,
        scratch_shapes=scratch,
        compiler_params=pltpu.CompilerParams(
            collective_id=0, has_side_effects=True, vmem_limit_bytes=58 * 2**20),
        name="ttt",
    )(key_rows, value_rows, token_rates.reshape(1, 384), query_rows, fast_gate, fast_up, fast_down.T)


def solution(mesh):
    placed = (
        P("ctx", None), P("ctx", None), P("ctx"), P("ctx", None),
        P("ctx", "state"), P("ctx", "state"), P("state", "ctx"),
    )
    return jax.shard_map(
        on_device, mesh=mesh, in_specs=placed, out_specs=P("ctx", "state"), check_vma=False)
```

```python
import functools

import jax
import jax.numpy as jnp
from jax import lax
from jax.experimental import pallas as pl
from jax.experimental.pallas import tpu as pltpu
from jax.sharding import PartitionSpec as P

MESH = pl.DeviceIdType.MESH
EPS = 1e-06
RATE = 0.5
NT = (((1,), (1,)), ((), ()))
NN = (((1,), (0,)), ((), ()))
F32, BF16 = jnp.float32, jnp.bfloat16
N_SEM = 224


def dot(a, b, dims):
    return lax.dot_general(a, b, dims, preferred_element_type=F32)


def place(x, y, z, k):
    return (x * 8 + (z % 2) * 4 + y, (z // 2) * 2 + k)


class Links:
    def __init__(self, send_sem, recv_sem):
        self.send_sem, self.recv_sem, self.used, self.sent = send_sem, recv_sem, 0, []

    def ids(self, count=1):
        first = self.used
        self.used += count
        assert self.used <= N_SEM
        return first

    def send(self, index, src, dst, device):
        copy = pltpu.make_async_remote_copy(
            src_ref=src, dst_ref=dst, send_sem=self.send_sem.at[index], recv_sem=self.recv_sem.at[index],
            device_id=device, device_id_type=MESH)
        copy.start()
        self.sent.append(copy)

    def wait(self, index, dst, device):
        pltpu.make_async_remote_copy(
            src_ref=dst, dst_ref=dst, send_sem=self.send_sem.at[index], recv_sem=self.recv_sem.at[index],
            device_id=device, device_id_type=MESH).wait_recv()

    def drain(self):
        for copy in self.sent:
            copy.wait_send()


def kernel(key_ref, val_ref, rate_ref, qry_ref, gate_ref, up_ref, down_ref, out_ref,
           key_all, val_all, qry_all, rates, rate_row, raw, w, gp, uq, hid, grads,
           d, ry0, x1a0, x1b0, x2a0, x2b0, x1a, x1b, x2a, x2b, es, ry, new,
           act, ob, osib, r, ryo, slot0, slots, fin, fins, yfin,
           send_sem, recv_sem, local_sem):
    c, s = lax.axis_index("ctx"), lax.axis_index("state")
    x, zlo, y = c // 8, (c // 4) % 2, c % 4
    zhi, k = s // 2, s % 2
    z = 2 * zhi + zlo
    p, yb = y // 2, y % 2
    xp, xm, xo = (x + 1) % 4, (x + 3) % 4, (x + 2) % 4
    zp, zm = (z + 1) % 8, (z + 7) % 8
    yt = y + 1 - 2 * yb
    yr = 3 - y
    po = 1 - p
    y2 = ((y + 1) // 2) % 2
    links = Links(send_sem, recv_sem)
    z_pair = z + 1 - 2 * zlo
    dev_xp, dev_xm = place(xp, y, z, k), place(xm, y, z, k)
    dev_yt, dev_yr = place(x, yt, z, k), place(x, yr, z, k)
    dev_zp, dev_zm = place(x, y, zp, k), place(x, y, zm, k)
    dev_core = place(x, y, z, 1 - k)
    dev_pair, dev_diag = place(x, y, z_pair, k), place(x, yt, z_pair, k)

    barrier = pltpu.get_barrier_semaphore()
    for other in (dev_xp, dev_xm, dev_yt, dev_yr, dev_zp, dev_zm, dev_diag, dev_core):
        pl.semaphore_signal(barrier, inc=1, device_id=other, device_id_type=MESH)

    def block(yy, zz):
        return 2 * yy + zz

    me = block(yb, zlo)

    full = [key_all, val_all, qry_all]
    src = [key_ref, val_ref, qry_ref]
    weights = [gate_ref, up_ref, down_ref]

    def share(a, qz, q2):
        return weights[a].at[:, pl.ds(pl.multiple_of((qz * 2 + q2) * 384, 128), 384)]

    stay = []
    for a in range(3):
        copy = pltpu.make_async_copy(share(a, zlo, y2), raw.at[c, a], local_sem.at[a])
        copy.start()
        stay.append(copy)
    rate_copy = pltpu.make_async_copy(rate_ref, rate_row, local_sem.at[6])
    rate_copy.start()
    local = []
    for i in range(3):
        copy = pltpu.make_async_copy(
            src[i], full[i].at[pl.ds(pl.multiple_of(me * 384, 16), 384)], local_sem.at[3 + i])
        copy.start()
        local.append(copy)
    pl.semaphore_wait(barrier, 8)

    st = {(a, j): links.ids() for a in range(3) for j in (1, 2, 3)}
    for a in range(3):
        links.send(st[a, 3], share(a, 1 - zlo, 1 - y2), raw.at[c, a], dev_diag)
        links.send(st[a, 1], share(a, zlo, 1 - y2), raw.at[c, a], dev_yt)
        links.send(st[a, 2], share(a, 1 - zlo, y2), raw.at[c, a], dev_pair)

    blocks = {"a": block(1 - yb, zlo), "b": block(yb, 1 - zlo), "c": block(1 - yb, 1 - zlo)}
    fine = [[(0, 16), (16, 32), (96, 48), (48, 48), (144, 48)],
            [(0, 48), (96, 48), (48, 32), (144, 32), (80, 16), (176, 16)],
            [(0, 96), (96, 96)]]
    coarse = [(0, 96), (96, 96)]

    def parts(i, kind):
        return coarse if kind == "b" else fine[i]

    tok_ids = {(i, kind, h): links.ids() for i in range(3) for kind in "abc" for h in parts(i, kind)}
    sib_ids = {(i, kind, h): links.ids() for i in range(3) for kind in "abc" for h in parts(i, kind)}

    def rows(i, b, h, kk=k):
        return full[i].at[pl.ds(pl.multiple_of(b * 384 + kk * 192 + h[0], 16), h[1])]

    z_to = [dev_zp, dev_zm]

    def a_start(i, h):
        mine = src[i].at[pl.ds(pl.multiple_of(k * 192 + h[0], 16), h[1])]
        links.send(tok_ids[i, "a", h], mine, rows(i, me, h), dev_yt)

    def b_start(i):
        for h in coarse:
            mine = src[i].at[pl.ds(pl.multiple_of(k * 192 + h[0], 16), h[1])]
            links.send(tok_ids[i, "b", h], mine, rows(i, me, h), z_to[h[0] // 96])

    def token_pass(i, kind, hs=None):
        for h in hs or parts(i, kind):
            here = rows(i, blocks[kind], h)
            links.wait(tok_ids[i, kind, h], here, dev_core)
            if kind == "a":
                links.send(tok_ids[i, "c", h], here, here, z_to[h[0] // 96])
            links.send(sib_ids[i, kind, h], here, here, dev_core)

    queue = [(i, h) for i in range(2) for h in fine[i]]

    def a_pass(n, ahead=3):
        i, h = queue[n]
        here = rows(i, blocks["a"], h)
        links.wait(tok_ids[i, "a", h], here, dev_core)
        if n + ahead < len(queue):
            a_start(*queue[n + ahead])
        links.send(tok_ids[i, "c", h], here, here, z_to[h[0] // 96])
        links.send(sib_ids[i, "a", h], here, here, dev_core)

    def token_finish(i, kinds="abc"):
        for kind in kinds:
            for h in parts(i, kind):
                links.wait(sib_ids[i, kind, h], rows(i, blocks[kind], h, 1 - k), dev_core)

    def gather(late, piece, half):
        ids = {}

        def at(name, j):
            if (name, j) not in ids:
                ids[name, j] = links.ids()
            return ids[name, j]

        def move(name, j, ref, device):
            links.send(at(name, j), ref, ref, device)

        def start(j, along_y=True):
            if along_y:
                move("y", j, piece(j, x, 0), dev_yr)
            move("xp", j, piece(j, x, 0), dev_xp)
            move("xm", j, piece(j, x, 0), dev_xm)

        def start_y(j):
            move("y", j, piece(j, x, 0), dev_yr)

        def cross(j):
            links.wait(at("y", j), piece(j, x, 1), dev_yr)
            move("xp2", j, piece(j, x, 1), dev_xp)
            move("xm2", j, piece(j, x, 1), dev_xm)

        def onward(j, other=0):
            which = "2" if other else ""
            links.wait(at("xp" + which, j), piece(j, xm, other), dev_xm)
            move("fp" + which, j, half(j, xm, other, 0), dev_xp)
            if j in late:
                move("y1", j, piece(j, xm, 0), dev_yr)
            links.wait(at("xm" + which, j), piece(j, xp, other), dev_xp)
            move("fm" + which, j, half(j, xp, other, 1), dev_xm)
            if j in late:
                move("y2", j, piece(j, xp, 0), dev_yr)

        def far(j, other=0):
            which = "2" if other else ""
            links.wait(at("fp" + which, j), half(j, xo, other, 0), dev_xm)
            links.wait(at("fm" + which, j), half(j, xo, other, 1), dev_xp)
            if j in late:
                move("y3", j, piece(j, xo, 0), dev_yr)

        def finish(j):
            if j in late:
                links.wait(at("y", j), piece(j, x, 1), dev_yr)
                links.wait(at("y1", j), piece(j, xm, 1), dev_yr)
                links.wait(at("y2", j), piece(j, xp, 1), dev_yr)
                links.wait(at("y3", j), piece(j, xo, 1), dev_yr)
            else:
                far(j, 1)

        return start, start_y, cross, onward, far, finish

    def source(j, xx, other):
        yy = yt if j % 2 else y
        return xx * 8 + (1 - zlo if j >= 2 else zlo) * 4 + (3 - yy if other else yy)

    def w_piece(j, xx, other):
        return raw.at[source(j, xx, other)]

    def w_half(j, xx, other, h):
        return raw.at[source(j, xx, other), :, pl.ds(16 * h, 16)]

    w_start, w_start_y, w_cross, w_onward, w_far, w_finish = gather((2,), w_piece, w_half)
    for copy in stay:
        copy.wait()
    w_start(0)
    for n in range(3):
        a_start(*queue[n])
    b_start(0)
    rate_copy.wait()
    rate_id = links.ids(3)

    def rate_at(b):
        return rates.at[:, pl.ds(pl.multiple_of(b * 384, 128), 384)]

    rate_at(me)[...] = rate_row[...].reshape(1, 384)
    links.send(rate_id, rate_at(me), rate_at(me), dev_yt)
    links.send(rate_id + 1, rate_at(me), rate_at(me), dev_pair)
    links.send(rate_id + 2, rate_at(me), rate_at(me), dev_diag)

    def w_arrived(j):
        for a in range(3):
            links.wait(st[a, j], raw.at[source(j, x, 0), a], dev_core)
        w_start(j, j != 2)

    w_onward(0)
    w_cross(0)
    w_arrived(1)
    w_arrived(3)
    w_arrived(2)
    a_pass(0)
    w_onward(0, 1)
    a_pass(1)
    a_pass(2)
    w_cross(1)
    w_cross(3)
    w_start_y(2)
    a_pass(3)
    token_pass(0, "b")
    b_start(1)
    w_onward(2)
    w_onward(1)
    w_onward(3)
    a_pass(4)
    w_onward(1, 1)
    a_pass(5)
    a_pass(6)
    w_far(2)
    a_pass(7)
    w_onward(3, 1)
    token_pass(0, "c")
    token_pass(1, "b")
    a_pass(8)
    for copy in local:
        copy.wait()
    for i, b in enumerate(("a", "b", "c")):
        links.wait(rate_id + i, rate_at(blocks[b]), dev_core)

    def upright(zz):
        for a in range(3):
            for xx in range(4):
                g = 2 * xx + zz
                w[a, :, pl.ds(pl.multiple_of(128 * g, 128), 128)] = (
                    raw[pl.ds(4 * g, 4), a].reshape(128, 384).astype(F32).T.astype(BF16))

    for j in (0, 1):
        w_far(j)
        w_finish(j)
    upright(zlo)
    a_pass(9)
    w_far(3)
    w_finish(3)
    a_pass(10)
    w_finish(2)
    upright(1 - zlo)

    def forward(yy):
        cols = pl.ds(pl.multiple_of(yy * 768, 256), 768)
        keys = key_all[cols, :]
        gate_pre = dot(w[0], keys, NT)
        up_pre = dot(w[1], keys, NT)
        gp[:, cols] = gate_pre
        uq[:, cols] = up_pre
        hid[:, cols] = (gate_pre * jax.nn.sigmoid(gate_pre) * up_pre * rates[:, cols]).astype(BF16)

    def backward(yy):
        cols = pl.ds(pl.multiple_of(yy * 768, 256), 768)
        back = dot(w[2], val_all[cols, :], NT) * rates[:, cols]
        gate_pre, up_pre = gp[:, cols], uq[:, cols]
        sig = jax.nn.sigmoid(gate_pre)
        grads[0, :, cols] = (back * up_pre * sig * (1.0 + gate_pre * (1.0 - sig))).astype(BF16)
        grads[1, :, cols] = (back * gate_pre * sig).astype(BF16)

    token_finish(0, "b")
    forward(yb)
    token_pass(1, "c")
    token_finish(0, "ac")
    forward(1 - yb)
    token_finish(1, "b")
    backward(yb)
    token_finish(1, "ac")
    for h in fine[2]:
        a_start(2, h)
    b_start(2)

    def direction(a, acts, tokens):
        d[a] = dot(acts[...], tokens[...], NN).reshape(4, 2, 48, 1024).astype(BF16)

    rs = {name: links.ids(3) for name in ("ap", "bm", "p", "m", "p2", "m2", "y")}
    ab = [pl.ds(0, 512), pl.ds(512, 512)]

    def reduce_start(a):
        links.send(rs["ap"] + a, d.at[a, xo, :, :, ab[0]], x1a.at[a - 1], dev_xp)
        links.send(rs["bm"] + a, d.at[a, xo, :, :, ab[1]], x1b.at[a - 1], dev_xm)

    def reduce_merge(a):
        links.wait(rs["ap"] + a, x1a.at[a - 1], dev_xm)
        d[a, xp, :, :, ab[0]] = d[a, xp, :, :, ab[0]] + x1a[a - 1]
        links.send(rs["p"] + a, d.at[a, xp, po], x2a.at[a - 1, po], dev_xp)
        links.wait(rs["bm"] + a, x1b.at[a - 1], dev_xp)
        d[a, xm, :, :, ab[1]] = d[a, xm, :, :, ab[1]] + x1b[a - 1]
        links.send(rs["m"] + a, d.at[a, xm, po], x2b.at[a - 1, po], dev_xm)

    def reduce_own(a):
        links.send(rs["p2"] + a, d.at[a, xp, p], x2a.at[a - 1, p], dev_xp)
        links.send(rs["m2"] + a, d.at[a, xm, p], x2b.at[a - 1, p], dev_xm)

    def row_total(a, pp):
        return d[a, x, pp].astype(F32) + x2a[a - 1, pp].astype(F32) + x2b[a - 1, pp].astype(F32)

    def reduce_cross(a):
        links.wait(rs["p"] + a, x2a.at[a - 1, po], dev_xm)
        links.wait(rs["m"] + a, x2b.at[a - 1, po], dev_xp)
        es[a - 1] = row_total(a, po).astype(BF16)
        links.send(rs["y"] + a, es.at[a - 1], ry.at[a - 1], dev_yr)

    def reduce_finish(a):
        links.wait(rs["p2"] + a, x2a.at[a - 1, p], dev_xm)
        links.wait(rs["m2"] + a, x2b.at[a - 1, p], dev_xp)
        links.wait(rs["y"] + a, ry.at[a - 1], dev_yr)
        renew(a, row_total(a, p) + ry[a - 1].astype(F32))

    def renew(a, grad):
        unit = pl.ds(pl.multiple_of((2 * x + p) * 48, 16), 48)
        old = w[a, unit, :].astype(F32)
        norm = jnp.sqrt(jnp.sum(old * old, axis=1, keepdims=True) + EPS)
        stepped = old + RATE * norm / jnp.sqrt(jnp.sum(grad * grad, axis=1, keepdims=True) + EPS) * grad
        scale = norm / jnp.sqrt(jnp.sum(stepped * stepped, axis=1, keepdims=True) + EPS)
        new[a, x, p] = (stepped * scale).astype(BF16)

    direction(2, hid, val_all)
    reduce_start(2)
    backward(1 - yb)
    direction(0, grads.at[0], key_all)
    cross_ids = links.ids(5)

    def cross_ref(n, ref, lead):
        if n < 2:
            return ref.at[lead + (xo,) + ((po,) if lead else ()) + (slice(None), ab[n])]
        return ref.at[lead + ((xp, xm, x)[n - 2],) + ((po,) if lead else ())]

    def cross_send(n):
        links.send(cross_ids + n, cross_ref(n, d, (0,)), cross_ref(n, ry0, ()), dev_yr)

    def cross_add(n):
        links.wait(cross_ids + n, cross_ref(n, ry0, ()), dev_yr)
        if n < 2:
            d[0, xo, p, :, ab[n]] = d[0, xo, p, :, ab[n]] + ry0[xo, :, ab[n]]
        else:
            to_x = (xp, xm, x)[n - 2]
            d[0, to_x, p] = d[0, to_x, p] + ry0[to_x]

    cross_send(0)
    cross_send(1)
    direction(1, grads.at[1], key_all)
    reduce_merge(2)
    reduce_start(1)
    cross_send(2)
    cross_send(3)
    token_pass(2, "b")
    cross_add(0)
    links.send(rs["ap"], d.at[0, xo, p, :, ab[0]], x1a0, dev_xp)
    cross_add(1)
    links.send(rs["bm"], d.at[0, xo, p, :, ab[1]], x1b0, dev_xm)
    reduce_own(2)
    reduce_cross(2)
    cross_send(4)
    reduce_merge(1)
    cross_add(2)
    links.wait(rs["ap"], x1a0, dev_xm)
    d[0, xp, p, :, ab[0]] = d[0, xp, p, :, ab[0]] + x1a0[...]
    links.send(rs["p"], d.at[0, xp, p], x2a0, dev_xp)
    cross_add(3)
    links.wait(rs["bm"], x1b0, dev_xp)
    d[0, xm, p, :, ab[1]] = d[0, xm, p, :, ab[1]] + x1b0[...]
    links.send(rs["m"], d.at[0, xm, p], x2b0, dev_xm)
    reduce_own(1)
    token_pass(2, "a")

    def n_piece(a, xx, other):
        return new.at[a, xx, po if other else p]

    def n_half(a, xx, other, h):
        return new.at[a, xx, po if other else p, :, ab[h]]

    n_start, n_start_y, n_cross, n_onward, n_far, n_finish = gather((1,), n_piece, n_half)
    reduce_cross(1)
    reduce_finish(2)
    n_start(2)
    cross_add(4)
    links.wait(rs["p"], x2a0, dev_xm)
    links.wait(rs["m"], x2b0, dev_xp)
    renew(0, d[0, x, p].astype(F32) + x2a0[...].astype(F32) + x2b0[...].astype(F32))
    n_start(0)
    reduce_finish(1)
    n_start(1)
    token_pass(2, "c")
    n_onward(2)
    n_cross(2)
    n_onward(0)
    n_cross(0)
    n_onward(1)
    n_onward(2, 1)
    n_onward(0, 1)
    n_far(1)
    token_finish(2)
    n_far(2)
    n_far(0)
    n_finish(2)
    n_finish(0)

    core_ids = links.ids(4)
    y_ids = {(i, j): links.ids() for i in range(2) for j in range(4)}
    lo, hi = pl.ds(0, 192), pl.ds(192, 192)

    def queries(i):
        b = block(yb if i % 2 else 1 - yb, zlo if i < 2 else 1 - zlo)
        return qry_all[pl.ds(pl.multiple_of(b * 384, 16), 384), :]

    def gate(i):
        gate_next = dot(queries(i), new[0].reshape(384, 1024), NT)
        act[i] = gate_next * jax.nn.sigmoid(gate_next)

    def apply(i):
        up_next = dot(queries(i), new[1].reshape(384, 1024), NT)
        term = dot((act[i] * up_next).astype(BF16), new[2].reshape(384, 1024), NN)
        for zz in range(4):
            for kk in range(2):
                at = (2 * zz + kk) * 128
                ob[i, kk, zz] = term[:, at:at + 128].astype(BF16)
        links.send(core_ids + i, ob.at[i, 1 - k], osib.at[i], dev_core)

    def both_cores(i):
        links.wait(core_ids + i, osib.at[i], dev_core)
        r[i // 2, i % 2] = ob[i, k] + osib[i]

    streams = ("far", "own", "y")
    ring = {(kind, sign): links.ids(4) for kind in streams for sign in (1, -1)}

    def to(step, sign):
        return ((z + sign * (4 - step) + 8) % 8) // 2

    targets = [(to(0, 1), to(2, 1), to(2, -1), zhi), (to(1, 1), to(1, -1), to(3, 1), to(3, -1))]

    def y_send(i, js):
        for j in js:
            t = targets[i][j]
            links.send(y_ids[i, j], r.at[i, 0, t, lo], ryo.at[i, t], dev_yt)

    def y_add(i, js):
        for j in js:
            t = targets[i][j]
            links.wait(y_ids[i, j], ryo.at[i, t], dev_yt)
            r[i, 1, t, lo] = r[i, 1, t, lo] + ryo[i, t]

    def chunk(kind, step, sign, part):
        base = 0 if kind == "y" else 192
        return (step % 2, 0 if kind == "far" else 1, to(step, sign), pl.ds(base + part[0], part[1]))

    halves = {1: (0, 96), -1: (96, 96)}

    def slot(kind, sign, step):
        n = 2 * streams.index(kind) + (0 if sign > 0 else 1)
        return slot0.at[n] if step == 0 else slots.at[n, step - 1]

    def ring_send(kind, sign, step):
        part = halves[sign] if step == 0 else (0, 192)
        links.send(ring[kind, sign] + step, r.at[chunk(kind, step, sign, part)],
                   slot(kind, sign, step), dev_zp if sign > 0 else dev_zm)

    def ring_recv(kind, sign, step):
        got = slot(kind, sign, step)
        links.wait(ring[kind, sign] + step, got, dev_zm if sign > 0 else dev_zp)
        return got

    def ring_add(kind, sign, step):
        got = ring_recv(kind, sign, step)
        where = chunk(kind, step + 1, sign, halves[sign] if step == 0 else (0, 192))
        r[where] = r[where] + got[...]

    def ring_step(kind, step):
        for sign in (1, -1):
            if step:
                ring_add(kind, sign, step - 1)
            ring_send(kind, sign, step)

    def ring_total(kind, i, rows_at):
        got = [ring_recv(kind, sign, 3)[...].astype(F32) for sign in (1, -1)]
        return r[0, i, zhi, rows_at].astype(F32) + got[0] + got[1]

    for i in range(4):
        gate(i)
    n_finish(1)
    apply(0)
    apply(2)
    both_cores(0)
    y_send(0, (0,))
    ring_step("far", 0)
    apply(1)
    both_cores(2)
    y_send(1, (0, 1))
    y_send(0, (1, 2))
    apply(3)
    both_cores(1)
    ring_step("own", 0)
    y_add(0, (0,))
    ring_step("y", 0)
    y_send(1, (2, 3))
    y_send(0, (3,))
    ring_step("far", 1)
    both_cores(3)
    ring_step("own", 1)
    y_add(1, (0, 1))
    ring_step("y", 1)
    ring_step("far", 2)
    ring_step("own", 2)
    y_add(0, (1, 2))
    ring_step("y", 2)
    ring_step("far", 3)
    ring_step("own", 3)
    y_add(1, (2, 3))
    ring_step("y", 3)
    y_add(0, (3,))
    fins[...] = ring_total("far", 0, hi).astype(BF16)
    fin_id = links.ids()
    links.send(fin_id, fins, yfin, dev_yt)
    fin[...] = ring_total("own", 1, hi)
    out_ref[lo, :] = ring_total("y", 1, lo).astype(BF16)
    links.wait(fin_id, yfin, dev_yt)
    out_ref[hi, :] = (fin[...] + yfin[...].astype(F32)).astype(BF16)
    links.drain()


def on_device(key_rows, value_rows, token_rates, query_rows, fast_gate, fast_up, fast_down):
    any_spec = pl.BlockSpec(memory_space=pl.ANY)
    vmem = pl.BlockSpec(memory_space=pltpu.VMEM)
    V = pltpu.VMEM
    scratch = [
        V((1536, 1024), BF16), V((1536, 1024), BF16), V((1536, 1024), BF16), V((1, 1536), F32),
        V((384,), F32), V((32, 3, 32, 384), BF16), V((3, 384, 1024), BF16),
        V((384, 1536), F32), V((384, 1536), F32), V((384, 1536), BF16), V((2, 384, 1536), BF16),
        V((3, 4, 2, 48, 1024), BF16),
        V((4, 48, 1024), BF16), V((48, 512), BF16), V((48, 512), BF16), V((48, 1024), BF16), V((48, 1024), BF16),
        V((2, 2, 48, 512), BF16), V((2, 2, 48, 512), BF16), V((2, 2, 48, 1024), BF16), V((2, 2, 48, 1024), BF16),
        V((2, 48, 1024), BF16), V((2, 48, 1024), BF16),
        V((3, 4, 2, 48, 1024), BF16),
        V((4, 384, 384), F32), V((4, 2, 4, 384, 128), BF16), V((4, 4, 384, 128), BF16), V((2, 2, 4, 384, 128), BF16),
        V((2, 4, 192, 128), BF16),
        V((6, 96, 128), BF16), V((6, 3, 192, 128), BF16),
        V((192, 128), F32), V((192, 128), BF16), V((192, 128), BF16),
        pltpu.SemaphoreType.DMA((N_SEM,)), pltpu.SemaphoreType.DMA((N_SEM,)), pltpu.SemaphoreType.DMA((8,)),
    ]
    return pl.pallas_call(
        kernel,
        out_shape=jax.ShapeDtypeStruct((384, 128), BF16),
        in_specs=[any_spec, any_spec, any_spec, any_spec, any_spec, any_spec, any_spec],
        out_specs=vmem,
        scratch_shapes=scratch,
        compiler_params=pltpu.CompilerParams(
            collective_id=0, has_side_effects=True, vmem_limit_bytes=58 * 2**20),
        name="ttt",
    )(key_rows, value_rows, token_rates, query_rows, fast_gate, fast_up, fast_down.T)


def solution(mesh):
    placed = (
        P("ctx", None), P("ctx", None), P("ctx"), P("ctx", None),
        P("ctx", "state"), P("ctx", "state"), P("state", "ctx"),
    )
    return jax.shard_map(
        on_device, mesh=mesh, in_specs=placed, out_specs=P("ctx", "state"), check_vma=False)
```

```python
import functools

import jax
import jax.numpy as jnp
from jax import lax
from jax.experimental import pallas as pl
from jax.experimental.pallas import tpu as pltpu
from jax.sharding import PartitionSpec as P

MESH = pl.DeviceIdType.MESH
EPS = 1e-06
RATE = 0.5
NT = (((1,), (1,)), ((), ()))
NN = (((1,), (0,)), ((), ()))
F32, BF16 = jnp.float32, jnp.bfloat16
N_SEND, N_RECV = 48, 171


def dot(a, b, dims):
    return lax.dot_general(a, b, dims, preferred_element_type=F32)


def place(x, y, z, k):
    return (x * 8 + (z % 2) * 4 + y, (z // 2) * 2 + k)


class Links:
    def __init__(self, send_sem, recv_sem):
        self.send_sem, self.recv_sem, self.used, self.sent, self.turn = send_sem, recv_sem, 0, [], 0

    def ids(self, count=1):
        first = self.used
        self.used += count
        assert self.used <= N_RECV
        return first

    def copy(self, index, src, dst, device, turn=0):
        return pltpu.make_async_remote_copy(
            src_ref=src, dst_ref=dst, send_sem=self.send_sem.at[turn], recv_sem=self.recv_sem.at[index],
            device_id=device, device_id_type=MESH)

    def send(self, index, src, dst, device):
        if len(self.sent) == N_SEND:
            self.drain(1)
        copy = self.copy(index, src, dst, device, self.turn % N_SEND)
        self.turn += 1
        copy.start()
        self.sent.append(copy)

    def wait(self, index, dst, device):
        self.copy(index, dst, dst, device).wait_recv()

    def drain(self, most=300, keep=0):
        count = max(0, min(most, len(self.sent) - keep))
        for copy in self.sent[:count]:
            copy.wait_send()
        del self.sent[:count]


def kernel(key_ref, val_ref, rate_ref, qry_ref, gate_ref, up_ref, down_ref, out_ref,
           key_all, val_all, qry_all, rates, rate_row, raw, w, gp, uq, hid, grads,
           d, ry0, x1a0, x1b0, x2a0, x2b0, x1a, x1b, x2a, x2b, es, ry, new,
           silu, act, ob, osib, r, ryo, slot0, slots, fin, yfin,
           send_sem, recv_sem, local_sem):
    c, s = lax.axis_index("ctx"), lax.axis_index("state")
    x, zlo, y = c // 8, (c // 4) % 2, c % 4
    zhi, k = s // 2, s % 2
    z = 2 * zhi + zlo
    p, yb = y // 2, y % 2
    xp, xm, xo = (x + 1) % 4, (x + 3) % 4, (x + 2) % 4
    zp, zm = (z + 1) % 8, (z + 7) % 8
    yt = y + 1 - 2 * yb
    yr = 3 - y
    po = 1 - p
    y2 = ((y + 1) // 2) % 2
    links = Links(send_sem, recv_sem)
    z_pair = z + 1 - 2 * zlo
    dev_xp, dev_xm = place(xp, y, z, k), place(xm, y, z, k)
    dev_yt, dev_yr = place(x, yt, z, k), place(x, yr, z, k)
    dev_zp, dev_zm = place(x, y, zp, k), place(x, y, zm, k)
    dev_core = place(x, y, z, 1 - k)
    dev_pair, dev_diag = place(x, y, z_pair, k), place(x, yt, z_pair, k)
    dev_yt_zp, dev_yt_zm = place(x, yt, zp, k), place(x, yt, zm, k)

    barrier = pltpu.get_barrier_semaphore()
    for other in (dev_xp, dev_xm, dev_yt, dev_yr, dev_zp, dev_zm, dev_yt_zp, dev_yt_zm, dev_core):
        pl.semaphore_signal(barrier, inc=1, device_id=other, device_id_type=MESH)

    def block(yy, zz):
        return 2 * yy + zz

    me = block(yb, zlo)

    full = [key_all, val_all, qry_all]
    src = [key_ref, val_ref, qry_ref]
    weights = [gate_ref, up_ref, down_ref]

    def share(a, qz, q2):
        return weights[a].at[:, pl.ds(pl.multiple_of((qz * 2 + q2) * 384, 128), 384)]

    stay = []
    for a in range(3):
        copy = pltpu.make_async_copy(share(a, zlo, y2), raw.at[c, a], local_sem.at[a])
        copy.start()
        stay.append(copy)
    rate_copy = pltpu.make_async_copy(rate_ref, rate_row, local_sem.at[6])
    rate_copy.start()
    local = []
    for i in range(3):
        copy = pltpu.make_async_copy(
            src[i], full[i].at[pl.ds(pl.multiple_of(me * 384, 16), 384)], local_sem.at[3 + i])
        copy.start()
        local.append(copy)
    pl.semaphore_wait(barrier, 9)

    st = {j: links.ids() for j in (1, 2, 3)}
    for a in range(3):
        links.send(st[3], share(a, 1 - zlo, 1 - y2), raw.at[c, a], dev_diag)
        links.send(st[2], share(a, 1 - zlo, y2), raw.at[c, a], dev_pair)
    for a in range(3):
        links.send(st[1], share(a, zlo, 1 - y2), raw.at[c, a], dev_yt)

    blocks = {"a": block(1 - yb, zlo), "b": block(yb, 1 - zlo), "c": block(1 - yb, 1 - zlo)}
    fine = [[(0, 16), (16, 32), (96, 48), (48, 48), (144, 48)],
            [(0, 48), (96, 48), (48, 32), (144, 32), (80, 16), (176, 16)],
            [(0, 96), (96, 96)]]
    coarse = [(0, 96), (96, 96)]

    def parts(i, kind):
        return coarse if kind == "b" else fine[i]

    tok_ids = {(i, kind, h): links.ids() for i in range(3) for kind in "abc" for h in parts(i, kind)}
    sib_ids = {(i, kind): links.ids() for i in range(3) for kind in "abc"}

    def rows(i, b, h, kk=k):
        return full[i].at[pl.ds(pl.multiple_of(b * 384 + kk * 192 + h[0], 16), h[1])]

    z_to = [dev_zp, dev_zm]

    def a_start(i, h):
        mine = src[i].at[pl.ds(pl.multiple_of(k * 192 + h[0], 16), h[1])]
        links.send(tok_ids[i, "a", h], mine, rows(i, me, h), dev_yt)

    def b_start(i):
        for h in coarse:
            mine = src[i].at[pl.ds(pl.multiple_of(k * 192 + h[0], 16), h[1])]
            links.send(tok_ids[i, "b", h], mine, rows(i, me, h), z_to[h[0] // 96])

    def token_pass(i, kind, hs=None):
        for h in hs or parts(i, kind):
            here = rows(i, blocks[kind], h)
            links.wait(tok_ids[i, kind, h], here, dev_core)
            if kind == "a":
                links.send(tok_ids[i, "c", h], here, here, z_to[h[0] // 96])
            links.send(sib_ids[i, kind], here, here, dev_core)

    queue = [(i, h) for i in range(2) for h in fine[i]]

    def a_pass(n, ahead=3):
        i, h = queue[n]
        here = rows(i, blocks["a"], h)
        links.wait(tok_ids[i, "a", h], here, dev_core)
        if n + ahead < len(queue):
            a_start(*queue[n + ahead])
        links.send(tok_ids[i, "c", h], here, here, z_to[h[0] // 96])
        links.send(sib_ids[i, "a"], here, here, dev_core)

    def token_finish(i, kinds="abc"):
        for kind in kinds:
            links.wait(sib_ids[i, kind], rows(i, blocks[kind], (0, 192), 1 - k), dev_core)

    def gather(late, piece, half):
        ids = {}

        def at(name, j):
            if (name, j) not in ids:
                ids[name, j] = links.ids()
            return ids[name, j]

        def move(name, j, ref, device):
            links.send(at(name, j), ref, ref, device)

        def start(j, along_y=True):
            if along_y:
                move("y", j, piece(j, x, 0), dev_yr)
            move("xp", j, piece(j, x, 0), dev_xp)
            move("xm", j, piece(j, x, 0), dev_xm)

        def start_y(j):
            move("y", j, piece(j, x, 0), dev_yr)

        def cross(j):
            links.wait(at("y", j), piece(j, x, 1), dev_yr)
            move("xp2", j, piece(j, x, 1), dev_xp)
            move("xm2", j, piece(j, x, 1), dev_xm)

        def onward(j, other=0):
            which = "2" if other else ""
            links.wait(at("xp" + which, j), piece(j, xm, other), dev_xm)
            move("fp" + which, j, half(j, xm, other, 0), dev_xp)
            if j in late:
                move("y1", j, piece(j, xm, 0), dev_yr)
            links.wait(at("xm" + which, j), piece(j, xp, other), dev_xp)
            move("fm" + which, j, half(j, xp, other, 1), dev_xm)
            if j in late:
                move("y2", j, piece(j, xp, 0), dev_yr)

        def far(j, other=0):
            which = "2" if other else ""
            links.wait(at("fp" + which, j), half(j, xo, other, 0), dev_xm)
            links.wait(at("fm" + which, j), half(j, xo, other, 1), dev_xp)
            if j in late:
                move("y3", j, piece(j, xo, 0), dev_yr)

        def finish(j):
            if j in late:
                links.wait(at("y", j), piece(j, x, 1), dev_yr)
                links.wait(at("y1", j), piece(j, xm, 1), dev_yr)
                links.wait(at("y2", j), piece(j, xp, 1), dev_yr)
                links.wait(at("y3", j), piece(j, xo, 1), dev_yr)
            else:
                far(j, 1)

        return start, start_y, cross, onward, far, finish

    def source(j, xx, other):
        yy = yt if j % 2 else y
        return xx * 8 + (1 - zlo if j >= 2 else zlo) * 4 + (3 - yy if other else yy)

    def w_piece(j, xx, other):
        return raw.at[source(j, xx, other)]

    def w_half(j, xx, other, h):
        return raw.at[source(j, xx, other), :, pl.ds(16 * h, 16)]

    w_start, w_start_y, w_cross, w_onward, w_far, w_finish = gather((2,), w_piece, w_half)
    for copy in stay:
        copy.wait()
    w_start(0)
    for n in range(3):
        a_start(*queue[n])
    b_start(0)
    rate_copy.wait()
    rate_id = links.ids(3)

    def rate_at(b):
        return rates.at[:, pl.ds(pl.multiple_of(b * 384, 128), 384)]

    rate_at(me)[...] = rate_row[...].reshape(1, 384)
    links.send(rate_id, rate_at(me), rate_at(me), dev_yt)
    links.send(rate_id + 1, rate_at(me), rate_at(me), dev_pair)
    links.send(rate_id + 2, rate_at(me), rate_at(me), dev_diag)

    def w_arrived(j):
        links.wait(st[j], raw.at[source(j, x, 0)], dev_core)
        w_start(j, j != 2)

    w_onward(0)
    w_cross(0)
    w_arrived(1)
    w_arrived(3)
    w_arrived(2)
    a_pass(0)
    w_onward(0, 1)
    a_pass(1)
    a_pass(2)
    w_cross(1)
    w_cross(3)
    w_start_y(2)
    a_pass(3)
    token_pass(0, "b")
    b_start(1)
    w_onward(2)
    w_onward(1)
    w_onward(3)
    a_pass(4)
    w_onward(1, 1)
    w_onward(3, 1)
    w_far(2)
    a_pass(5)
    a_pass(6)
    token_pass(0, "c", fine[0][:2])
    a_pass(7)
    token_pass(0, "c", fine[0][2:])
    token_pass(1, "b")
    for copy in local:
        copy.wait()
    for i, b in enumerate(("a", "b", "c")):
        links.wait(rate_id + i, rate_at(blocks[b]), dev_core)

    def upright(zz):
        for a in range(3):
            for xx in range(4):
                g = 2 * xx + zz
                w[a, :, pl.ds(pl.multiple_of(128 * g, 128), 128)] = (
                    raw[pl.ds(4 * g, 4), a].reshape(128, 384).astype(F32).T.astype(BF16))

    for j in (0, 1):
        w_far(j)
        w_finish(j)
    upright(zlo)
    w_far(3)
    w_finish(3)
    w_finish(2)
    a_pass(8)
    upright(1 - zlo)
    a_pass(9)
    a_pass(10)

    def forward(yy):
        cols = pl.ds(pl.multiple_of(yy * 768, 256), 768)
        keys = key_all[cols, :]
        gate_pre = dot(w[0], keys, NT)
        up_pre = dot(w[1], keys, NT)
        gp[:, cols] = gate_pre
        uq[:, cols] = up_pre
        hid[:, cols] = (gate_pre * jax.nn.sigmoid(gate_pre) * up_pre * rates[:, cols]).astype(BF16)

    def backward(yy):
        cols = pl.ds(pl.multiple_of(yy * 768, 256), 768)
        back = dot(w[2], val_all[cols, :], NT) * rates[:, cols]
        gate_pre, up_pre = gp[:, cols], uq[:, cols]
        sig = jax.nn.sigmoid(gate_pre)
        grads[0, :, cols] = (back * up_pre * sig * (1.0 + gate_pre * (1.0 - sig))).astype(BF16)
        grads[1, :, cols] = (back * gate_pre * sig).astype(BF16)

    token_finish(0, "b")
    forward(yb)
    token_pass(1, "c", fine[1][:3])
    token_finish(0, "ac")
    forward(1 - yb)
    token_pass(1, "c", fine[1][3:])
    token_finish(1, "b")
    backward(yb)
    token_finish(1, "ac")
    for h in fine[2]:
        a_start(2, h)
    b_start(2)

    def direction(a, acts, tokens):
        d[a] = dot(acts[...], tokens[...], NN).reshape(4, 2, 48, 1024).astype(BF16)

    rs = {name: links.ids(3) for name in ("ap", "bm", "p", "m", "p2", "m2", "y")}
    ab = [pl.ds(0, 512), pl.ds(512, 512)]

    def reduce_start(a):
        links.send(rs["ap"] + a, d.at[a, xo, :, :, ab[0]], x1a.at[a - 1], dev_xp)
        links.send(rs["bm"] + a, d.at[a, xo, :, :, ab[1]], x1b.at[a - 1], dev_xm)

    def reduce_merge(a):
        links.wait(rs["ap"] + a, x1a.at[a - 1], dev_xm)
        d[a, xp, :, :, ab[0]] = d[a, xp, :, :, ab[0]] + x1a[a - 1]
        links.send(rs["p"] + a, d.at[a, xp, po], x2a.at[a - 1, po], dev_xp)
        links.wait(rs["bm"] + a, x1b.at[a - 1], dev_xp)
        d[a, xm, :, :, ab[1]] = d[a, xm, :, :, ab[1]] + x1b[a - 1]
        links.send(rs["m"] + a, d.at[a, xm, po], x2b.at[a - 1, po], dev_xm)

    def reduce_own(a):
        links.send(rs["p2"] + a, d.at[a, xp, p], x2a.at[a - 1, p], dev_xp)
        links.send(rs["m2"] + a, d.at[a, xm, p], x2b.at[a - 1, p], dev_xm)

    def row_total(a, pp):
        return d[a, x, pp].astype(F32) + x2a[a - 1, pp].astype(F32) + x2b[a - 1, pp].astype(F32)

    def reduce_cross(a):
        links.wait(rs["p"] + a, x2a.at[a - 1, po], dev_xm)
        links.wait(rs["m"] + a, x2b.at[a - 1, po], dev_xp)
        es[a - 1] = row_total(a, po).astype(BF16)
        links.send(rs["y"] + a, es.at[a - 1], ry.at[a - 1], dev_yr)

    def reduce_finish(a):
        links.wait(rs["p2"] + a, x2a.at[a - 1, p], dev_xm)
        links.wait(rs["m2"] + a, x2b.at[a - 1, p], dev_xp)
        links.wait(rs["y"] + a, ry.at[a - 1], dev_yr)
        renew(a, row_total(a, p) + ry[a - 1].astype(F32))

    def renew(a, grad):
        unit = pl.ds(pl.multiple_of((2 * x + p) * 48, 16), 48)
        old = w[a, unit, :].astype(F32)
        norm = jnp.sqrt(jnp.sum(old * old, axis=1, keepdims=True) + EPS)
        stepped = old + RATE * norm / jnp.sqrt(jnp.sum(grad * grad, axis=1, keepdims=True) + EPS) * grad
        scale = norm / jnp.sqrt(jnp.sum(stepped * stepped, axis=1, keepdims=True) + EPS)
        new[a, x, p] = (stepped * scale).astype(BF16)

    direction(2, hid, val_all)
    reduce_start(2)
    backward(1 - yb)
    direction(1, grads.at[1], key_all)
    reduce_start(1)
    cross_ids = links.ids(5)

    def cross_ref(n, ref, lead):
        if n < 2:
            return ref.at[lead + (xo,) + ((po,) if lead else ()) + (slice(None), ab[n])]
        return ref.at[lead + ((xp, xm, x)[n - 2],) + ((po,) if lead else ())]

    def cross_send(n):
        links.send(cross_ids + n, cross_ref(n, d, (0,)), cross_ref(n, ry0, ()), dev_yr)

    def cross_add(n):
        links.wait(cross_ids + n, cross_ref(n, ry0, ()), dev_yr)
        if n < 2:
            d[0, xo, p, :, ab[n]] = d[0, xo, p, :, ab[n]] + ry0[xo, :, ab[n]]
        else:
            to_x = (xp, xm, x)[n - 2]
            d[0, to_x, p] = d[0, to_x, p] + ry0[to_x]

    direction(0, grads.at[0], key_all)
    cross_send(0)
    cross_send(1)
    cross_send(2)
    reduce_merge(2)
    cross_send(3)
    links.drain(40, 25)
    reduce_merge(1)
    cross_add(0)
    links.send(rs["ap"], d.at[0, xo, p, :, ab[0]], x1a0, dev_xp)
    cross_add(1)
    links.send(rs["bm"], d.at[0, xo, p, :, ab[1]], x1b0, dev_xm)
    reduce_own(2)
    reduce_cross(2)
    cross_send(4)
    links.drain(25, 25)
    cross_add(2)
    links.drain(25, 25)
    reduce_cross(1)
    links.wait(rs["ap"], x1a0, dev_xm)
    d[0, xp, p, :, ab[0]] = d[0, xp, p, :, ab[0]] + x1a0[...]
    links.send(rs["p"], d.at[0, xp, p], x2a0, dev_xp)
    cross_add(3)
    links.wait(rs["bm"], x1b0, dev_xp)
    d[0, xm, p, :, ab[1]] = d[0, xm, p, :, ab[1]] + x1b0[...]
    links.send(rs["m"], d.at[0, xm, p], x2b0, dev_xm)
    reduce_own(1)
    token_pass(2, "b")
    token_pass(2, "a")

    def n_piece(a, xx, other):
        return new.at[a, xx, po if other else p]

    def n_half(a, xx, other, h):
        return new.at[a, xx, po if other else p, :, ab[h]]

    n_start, n_start_y, n_cross, n_onward, n_far, n_finish = gather((0,), n_piece, n_half)
    links.drain(25, 25)
    reduce_finish(2)
    n_start(2)
    links.drain(25, 25)
    cross_add(4)
    links.wait(rs["p"], x2a0, dev_xm)
    links.wait(rs["m"], x2b0, dev_xp)
    renew(0, d[0, x, p].astype(F32) + x2a0[...].astype(F32) + x2b0[...].astype(F32))
    n_start(0)
    links.drain(25, 25)
    reduce_finish(1)
    n_start(1)
    token_pass(2, "c")
    links.drain(25, 25)
    n_onward(2)
    links.drain(25, 20)
    n_onward(0)
    n_cross(1)
    n_onward(1)
    n_cross(2)
    links.drain(25, 15)
    n_far(0)
    links.drain(25, 12)
    n_onward(1, 1)
    token_finish(2)

    core_ids = links.ids(4)
    y_ids = {(i, j): links.ids() for i in range(2) for j in range(4)}
    lo, hi = pl.ds(0, 192), pl.ds(192, 192)

    def queries(i):
        b = block(yb if i % 2 else 1 - yb, zlo if i < 2 else 1 - zlo)
        return qry_all[pl.ds(pl.multiple_of(b * 384, 16), 384), :]

    def gate(i):
        gate_next = dot(queries(i), new[0].reshape(384, 1024), NT)
        silu[i] = gate_next * jax.nn.sigmoid(gate_next)

    def activate(i):
        act[i] = (silu[i] * dot(queries(i), new[1].reshape(384, 1024), NT)).astype(BF16)

    def apply(i):
        term = dot(act[i], new[2].reshape(384, 1024), NN)
        for zz in range(4):
            for kk in range(2):
                at = (2 * zz + kk) * 128
                ob[i, kk, zz] = term[:, at:at + 128].astype(BF16)
        links.send(core_ids + i, ob.at[i, 1 - k], osib.at[i], dev_core)

    def both_cores(i):
        links.wait(core_ids + i, osib.at[i], dev_core)
        r[i // 2, i % 2] = ob[i, k] + osib[i]

    streams = ("far", "own", "y")
    ring = {(kind, sign): links.ids(4) for kind in streams for sign in (1, -1)}

    def to(step, sign):
        return ((z + sign * (4 - step) + 8) % 8) // 2

    targets = [(to(0, 1), to(2, 1), to(2, -1), zhi), (to(1, 1), to(1, -1), to(3, 1), to(3, -1))]

    def y_send(i, js):
        for j in js:
            t = targets[i][j]
            links.send(y_ids[i, j], r.at[i, 0, t, lo], ryo.at[i, t], dev_yt)

    def y_add(i, js):
        for j in js:
            t = targets[i][j]
            links.wait(y_ids[i, j], ryo.at[i, t], dev_yt)
            r[i, 1, t, lo] = r[i, 1, t, lo] + ryo[i, t]

    def chunk(kind, step, sign, part):
        base = 0 if kind == "y" else 192
        return (step % 2, 0 if kind == "far" else 1, to(step, sign), pl.ds(base + part[0], part[1]))

    halves = {1: (0, 96), -1: (96, 96)}

    def slot(kind, sign, step):
        n = 2 * streams.index(kind) + (0 if sign > 0 else 1)
        return slot0.at[n] if step == 0 else slots.at[n, step - 1]

    def ring_send(kind, sign, step):
        part = halves[sign] if step == 0 else (0, 192)
        device = dev_zp if sign > 0 else dev_zm
        if kind == "far" and step == 3:
            device = dev_yt_zp if sign > 0 else dev_yt_zm
        links.send(ring[kind, sign] + step, r.at[chunk(kind, step, sign, part)], slot(kind, sign, step), device)

    def ring_recv(kind, sign, step):
        got = slot(kind, sign, step)
        links.wait(ring[kind, sign] + step, got, dev_zm if sign > 0 else dev_zp)
        return got

    def ring_add(kind, sign, step):
        got = ring_recv(kind, sign, step)
        where = chunk(kind, step + 1, sign, halves[sign] if step == 0 else (0, 192))
        r[where] = r[where] + got[...]

    def ring_step(kind, step):
        for sign in (1, -1):
            if step:
                ring_add(kind, sign, step - 1)
            ring_send(kind, sign, step)

    def ring_total(kind):
        got = [ring_recv(kind, sign, 3)[...].astype(F32) for sign in (1, -1)]
        return got[0] + got[1]

    n_finish(0)
    gate(0)
    gate(1)
    n_onward(2, 1)
    gate(2)
    gate(3)
    n_far(1)
    n_finish(1)
    for i in (0, 2, 1, 3):
        activate(i)
    n_far(2)
    n_finish(2)
    apply(0)
    apply(2)
    apply(1)
    both_cores(0)
    y_send(0, (0,))
    ring_step("far", 0)
    both_cores(2)
    y_send(1, (0, 1))
    y_send(0, (1, 2))
    apply(3)
    both_cores(1)
    ring_step("own", 0)
    links.drain(25, 12)
    y_add(0, (0,))
    ring_step("y", 0)
    y_send(1, (2, 3))
    y_send(0, (3,))
    fin_id = links.ids()
    links.send(fin_id, r.at[0, 0, zhi, hi], yfin, dev_yt)
    ring_step("far", 1)
    both_cores(3)
    links.drain(25, 12)
    y_add(1, (0, 1))
    ring_step("y", 1)
    ring_step("own", 1)
    ring_step("far", 2)
    y_add(0, (1, 2))
    links.drain(25, 12)
    ring_step("y", 2)
    ring_step("own", 2)
    ring_step("far", 3)
    y_add(1, (2, 3))
    links.drain(25, 10)
    ring_step("y", 3)
    ring_step("own", 3)
    y_add(0, (3,))
    links.drain(25, 6)
    links.wait(fin_id, yfin, dev_yt)
    fin[...] = r[0, 1, zhi, hi].astype(F32) + yfin[...].astype(F32) + ring_total("far")
    out_ref[hi, :] = (fin[...] + ring_total("own")).astype(BF16)
    out_ref[lo, :] = (r[0, 1, zhi, lo].astype(F32) + ring_total("y")).astype(BF16)
    links.drain()


def on_device(key_rows, value_rows, token_rates, query_rows, fast_gate, fast_up, fast_down):
    any_spec = pl.BlockSpec(memory_space=pl.ANY)
    vmem = pl.BlockSpec(memory_space=pltpu.VMEM)
    V = pltpu.VMEM
    scratch = [
        V((1536, 1024), BF16), V((1536, 1024), BF16), V((1536, 1024), BF16), V((1, 1536), F32),
        V((384,), F32), V((32, 3, 32, 384), BF16), V((3, 384, 1024), BF16),
        V((384, 1536), F32), V((384, 1536), F32), V((384, 1536), BF16), V((2, 384, 1536), BF16),
        V((3, 4, 2, 48, 1024), BF16),
        V((4, 48, 1024), BF16), V((48, 512), BF16), V((48, 512), BF16), V((48, 1024), BF16), V((48, 1024), BF16),
        V((2, 2, 48, 512), BF16), V((2, 2, 48, 512), BF16), V((2, 2, 48, 1024), BF16), V((2, 2, 48, 1024), BF16),
        V((2, 48, 1024), BF16), V((2, 48, 1024), BF16),
        V((3, 4, 2, 48, 1024), BF16),
        V((4, 384, 384), F32), V((4, 384, 384), BF16), V((4, 2, 4, 384, 128), BF16), V((4, 4, 384, 128), BF16), V((2, 2, 4, 384, 128), BF16),
        V((2, 4, 192, 128), BF16),
        V((6, 96, 128), BF16), V((6, 3, 192, 128), BF16),
        V((192, 128), F32), V((192, 128), BF16),
        pltpu.SemaphoreType.DMA((N_SEND,)), pltpu.SemaphoreType.DMA((N_RECV,)), pltpu.SemaphoreType.DMA((7,)),
    ]
    return pl.pallas_call(
        kernel,
        out_shape=jax.ShapeDtypeStruct((384, 128), BF16),
        in_specs=[any_spec, any_spec, any_spec, any_spec, any_spec, any_spec, any_spec],
        out_specs=vmem,
        scratch_shapes=scratch,
        compiler_params=pltpu.CompilerParams(
            collective_id=0, has_side_effects=True, vmem_limit_bytes=58 * 2**20),
        name="ttt",
    )(key_rows, value_rows, token_rates, query_rows, fast_gate, fast_up, fast_down.T)


def solution(mesh):
    placed = (
        P("ctx", None), P("ctx", None), P("ctx"), P("ctx", None),
        P("ctx", "state"), P("ctx", "state"), P("state", "ctx"),
    )
    return jax.shard_map(
        on_device, mesh=mesh, in_specs=placed, out_specs=P("ctx", "state"), check_vma=False)
```

```python
import functools

import jax
import jax.numpy as jnp
from jax import lax
from jax.experimental import pallas as pl
from jax.experimental.pallas import tpu as pltpu
from jax.sharding import PartitionSpec as P

MESH = pl.DeviceIdType.MESH
EPS = 1e-06
RATE = 0.5
NT = (((1,), (1,)), ((), ()))
NN = (((1,), (0,)), ((), ()))
F32, BF16 = jnp.float32, jnp.bfloat16
N_SEND, N_RECV = 32, 171
LOW = 192


def dot(a, b, dims):
    return lax.dot_general(a, b, dims, preferred_element_type=F32)


def place(x, y, z, k):
    return (x * 8 + (z % 2) * 4 + y, (z // 2) * 2 + k)


class Links:
    def __init__(self, send_sem, recv_sem):
        self.send_sem, self.recv_sem, self.used, self.sent, self.turn = send_sem, recv_sem, 0, [], 0

    def ids(self, count=1):
        first = self.used
        self.used += count
        assert self.used <= N_RECV
        return first

    def copy(self, index, src, dst, device, turn=0):
        return pltpu.make_async_remote_copy(
            src_ref=src, dst_ref=dst, send_sem=self.send_sem.at[turn], recv_sem=self.recv_sem.at[index],
            device_id=device, device_id_type=MESH)

    def send(self, index, src, dst, device):
        if len(self.sent) == N_SEND:
            self.drain(1)
        copy = self.copy(index, src, dst, device, self.turn % N_SEND)
        self.turn += 1
        copy.start()
        self.sent.append(copy)

    def wait(self, index, dst, device):
        self.copy(index, dst, dst, device).wait_recv()

    def drain(self, most=300, keep=0):
        count = max(0, min(most, len(self.sent) - keep))
        for copy in self.sent[:count]:
            copy.wait_send()
        del self.sent[:count]


def kernel(key_ref, val_ref, rate_ref, qry_ref, gate_ref, up_ref, down_ref, out_ref,
           key_all, val_all, qry_all, rates, rate_row, raw, w, gp, uq, hid, grads,
           d, ry0, x1a0, x1b0, x2a0, x2b0, x1a, x1b, x2a, x2b, es, ry, new,
           silu, act, ob, osib, r, ryo, slots, fin, yfin,
           send_sem, recv_sem, local_sem):
    c, s = lax.axis_index("ctx"), lax.axis_index("state")
    x, zlo, y = c // 8, (c // 4) % 2, c % 4
    zhi, k = s // 2, s % 2
    z = 2 * zhi + zlo
    p, yb = y // 2, y % 2
    xp, xm, xo = (x + 1) % 4, (x + 3) % 4, (x + 2) % 4
    zp, zm = (z + 1) % 8, (z + 7) % 8
    yt = y + 1 - 2 * yb
    yr = 3 - y
    po = 1 - p
    y2 = ((y + 1) // 2) % 2
    links = Links(send_sem, recv_sem)
    z_pair = z + 1 - 2 * zlo
    dev_xp, dev_xm = place(xp, y, z, k), place(xm, y, z, k)
    dev_yt, dev_yr = place(x, yt, z, k), place(x, yr, z, k)
    dev_zp, dev_zm = place(x, y, zp, k), place(x, y, zm, k)
    dev_core = place(x, y, z, 1 - k)
    dev_pair, dev_diag = place(x, y, z_pair, k), place(x, yt, z_pair, k)
    dev_yt_zp, dev_yt_zm = place(x, yt, zp, k), place(x, yt, zm, k)

    barrier = pltpu.get_barrier_semaphore()
    for other in (dev_xp, dev_xm, dev_yt, dev_yr, dev_zp, dev_zm, dev_yt_zp, dev_yt_zm, dev_core):
        pl.semaphore_signal(barrier, inc=1, device_id=other, device_id_type=MESH)

    def block(yy, zz):
        return 2 * yy + zz

    me = block(yb, zlo)

    full = [key_all, val_all, qry_all]
    src = [key_ref, val_ref, qry_ref]
    weights = [gate_ref, up_ref, down_ref]

    def share(a, qz, q2):
        return weights[a].at[:, pl.ds(pl.multiple_of((qz * 2 + q2) * 384, 128), 384)]

    stay = []
    for a in range(3):
        copy = pltpu.make_async_copy(share(a, zlo, y2), raw.at[c, a], local_sem.at[a])
        copy.start()
        stay.append(copy)
    rate_copy = pltpu.make_async_copy(rate_ref, rate_row, local_sem.at[6])
    rate_copy.start()
    local = []
    for i in range(3):
        copy = pltpu.make_async_copy(
            src[i], full[i].at[pl.ds(pl.multiple_of(me * 384, 16), 384)], local_sem.at[3 + i])
        copy.start()
        local.append(copy)
    pl.semaphore_wait(barrier, 9)

    st = {j: links.ids() for j in (1, 2, 3)}
    for a in range(3):
        links.send(st[3], share(a, 1 - zlo, 1 - y2), raw.at[c, a], dev_diag)
        links.send(st[2], share(a, 1 - zlo, y2), raw.at[c, a], dev_pair)
    for a in range(3):
        links.send(st[1], share(a, zlo, 1 - y2), raw.at[c, a], dev_yt)

    blocks = {"a": block(1 - yb, zlo), "b": block(yb, 1 - zlo), "c": block(1 - yb, 1 - zlo)}
    fine = [[(0, 16), (16, 32), (96, 48), (48, 48), (144, 48)],
            [(0, 48), (96, 48), (48, 32), (144, 32), (80, 16), (176, 16)],
            [(0, 96), (96, 96)]]
    coarse = [(0, 96), (96, 96)]

    def parts(i, kind):
        return coarse if kind == "b" else fine[i]

    tok_ids = {(i, kind, h): links.ids() for i in range(3) for kind in "abc" for h in parts(i, kind)}
    sib_ids = {(i, kind): links.ids() for i in range(3) for kind in "abc"}

    def rows(i, b, h, kk=k):
        return full[i].at[pl.ds(pl.multiple_of(b * 384 + kk * 192 + h[0], 16), h[1])]

    z_to = [dev_zp, dev_zm]

    def a_start(i, h):
        mine = src[i].at[pl.ds(pl.multiple_of(k * 192 + h[0], 16), h[1])]
        links.send(tok_ids[i, "a", h], mine, rows(i, me, h), dev_yt)

    def b_start(i):
        for h in coarse:
            mine = src[i].at[pl.ds(pl.multiple_of(k * 192 + h[0], 16), h[1])]
            links.send(tok_ids[i, "b", h], mine, rows(i, me, h), z_to[h[0] // 96])

    def token_pass(i, kind, hs=None):
        for h in hs or parts(i, kind):
            here = rows(i, blocks[kind], h)
            links.wait(tok_ids[i, kind, h], here, dev_core)
            if kind == "a":
                links.send(tok_ids[i, "c", h], here, here, z_to[h[0] // 96])
            links.send(sib_ids[i, kind], here, here, dev_core)

    queue = [(i, h) for i in range(2) for h in fine[i]]

    def a_pass(n, ahead=3):
        i, h = queue[n]
        here = rows(i, blocks["a"], h)
        links.wait(tok_ids[i, "a", h], here, dev_core)
        if n + ahead < len(queue):
            a_start(*queue[n + ahead])
        links.send(tok_ids[i, "c", h], here, here, z_to[h[0] // 96])
        links.send(sib_ids[i, "a"], here, here, dev_core)

    def token_finish(i, kinds="abc"):
        for kind in kinds:
            links.wait(sib_ids[i, kind], rows(i, blocks[kind], (0, 192), 1 - k), dev_core)

    def gather(late, piece, half):
        ids = {}

        def at(name, j):
            if (name, j) not in ids:
                ids[name, j] = links.ids()
            return ids[name, j]

        def move(name, j, ref, device):
            links.send(at(name, j), ref, ref, device)

        def start(j, along_y=True):
            if along_y:
                move("y", j, piece(j, x, 0), dev_yr)
            move("xp", j, piece(j, x, 0), dev_xp)
            move("xm", j, piece(j, x, 0), dev_xm)

        def start_y(j):
            move("y", j, piece(j, x, 0), dev_yr)

        def cross(j):
            links.wait(at("y", j), piece(j, x, 1), dev_yr)
            move("xp2", j, piece(j, x, 1), dev_xp)
            move("xm2", j, piece(j, x, 1), dev_xm)

        def onward(j, other=0):
            which = "2" if other else ""
            links.wait(at("xp" + which, j), piece(j, xm, other), dev_xm)
            move("fp" + which, j, half(j, xm, other, 0), dev_xp)
            if j in late:
                move("y1", j, piece(j, xm, 0), dev_yr)
            links.wait(at("xm" + which, j), piece(j, xp, other), dev_xp)
            move("fm" + which, j, half(j, xp, other, 1), dev_xm)
            if j in late:
                move("y2", j, piece(j, xp, 0), dev_yr)

        def far(j, other=0):
            which = "2" if other else ""
            links.wait(at("fp" + which, j), half(j, xo, other, 0), dev_xm)
            links.wait(at("fm" + which, j), half(j, xo, other, 1), dev_xp)
            if j in late:
                move("y3", j, piece(j, xo, 0), dev_yr)

        def finish(j):
            if j in late:
                links.wait(at("y", j), piece(j, x, 1), dev_yr)
                links.wait(at("y1", j), piece(j, xm, 1), dev_yr)
                links.wait(at("y2", j), piece(j, xp, 1), dev_yr)
                links.wait(at("y3", j), piece(j, xo, 1), dev_yr)
            else:
                far(j, 1)

        return start, start_y, cross, onward, far, finish

    def source(j, xx, other):
        yy = yt if j % 2 else y
        return xx * 8 + (1 - zlo if j >= 2 else zlo) * 4 + (3 - yy if other else yy)

    def w_piece(j, xx, other):
        return raw.at[source(j, xx, other)]

    def w_half(j, xx, other, h):
        return raw.at[source(j, xx, other), :, pl.ds(16 * h, 16)]

    w_start, w_start_y, w_cross, w_onward, w_far, w_finish = gather((2,), w_piece, w_half)
    for copy in stay:
        copy.wait()
    w_start(0)
    for n in range(3):
        a_start(*queue[n])
    b_start(0)
    rate_copy.wait()
    rate_id = links.ids(3)

    def rate_at(b):
        return rates.at[:, pl.ds(pl.multiple_of(b * 384, 128), 384)]

    rate_at(me)[...] = rate_row[...].reshape(1, 384)
    links.send(rate_id, rate_at(me), rate_at(me), dev_yt)
    links.send(rate_id + 1, rate_at(me), rate_at(me), dev_pair)
    links.send(rate_id + 2, rate_at(me), rate_at(me), dev_diag)

    def w_arrived(j):
        links.wait(st[j], raw.at[source(j, x, 0)], dev_core)
        w_start(j, j != 2)

    w_onward(0)
    w_cross(0)
    w_arrived(1)
    w_arrived(3)
    w_arrived(2)
    a_pass(0)
    w_onward(0, 1)
    a_pass(1)
    a_pass(2)
    w_cross(1)
    w_cross(3)
    w_start_y(2)
    a_pass(3)
    token_pass(0, "b")
    b_start(1)
    w_onward(2)
    w_onward(1)
    w_onward(3)
    a_pass(4)
    w_onward(1, 1)
    w_onward(3, 1)
    w_far(2)
    a_pass(5)
    a_pass(6)
    token_pass(0, "c", fine[0][:2])
    a_pass(7)
    token_pass(0, "c", fine[0][2:])
    token_pass(1, "b")
    for copy in local:
        copy.wait()
    for i, b in enumerate(("a", "b", "c")):
        links.wait(rate_id + i, rate_at(blocks[b]), dev_core)

    def upright(zz):
        for a in range(3):
            for xx in range(4):
                g = 2 * xx + zz
                w[a, :, pl.ds(pl.multiple_of(128 * g, 128), 128)] = (
                    raw[pl.ds(4 * g, 4), a].reshape(128, 384).astype(F32).T.astype(BF16))

    for j in (0, 1):
        w_far(j)
        w_finish(j)
    upright(zlo)
    w_far(3)
    w_finish(3)
    w_finish(2)
    a_pass(8)
    upright(1 - zlo)
    a_pass(9)
    a_pass(10)

    def forward(yy):
        cols = pl.ds(pl.multiple_of(yy * 768, 256), 768)
        keys = key_all[cols, :]
        gate_pre = dot(w[0], keys, NT)
        up_pre = dot(w[1], keys, NT)
        gp[:, cols] = gate_pre
        uq[:, cols] = up_pre
        hid[:, cols] = (gate_pre * jax.nn.sigmoid(gate_pre) * up_pre * rates[:, cols]).astype(BF16)

    def backward(yy):
        cols = pl.ds(pl.multiple_of(yy * 768, 256), 768)
        back = dot(w[2], val_all[cols, :], NT) * rates[:, cols]
        gate_pre, up_pre = gp[:, cols], uq[:, cols]
        sig = jax.nn.sigmoid(gate_pre)
        grads[0, :, cols] = (back * up_pre * sig * (1.0 + gate_pre * (1.0 - sig))).astype(BF16)
        grads[1, :, cols] = (back * gate_pre * sig).astype(BF16)

    token_finish(0, "b")
    forward(yb)
    token_pass(1, "c", fine[1][:3])
    token_finish(0, "ac")
    forward(1 - yb)
    token_pass(1, "c", fine[1][3:])
    token_finish(1, "b")
    backward(yb)
    token_finish(1, "ac")
    for h in fine[2]:
        a_start(2, h)
    b_start(2)

    def direction(a, acts, tokens):
        d[a] = dot(acts[...], tokens[...], NN).reshape(4, 2, 48, 1024).astype(BF16)

    rs = {name: links.ids(3) for name in ("ap", "bm", "p", "m", "p2", "m2", "y")}
    ab = [pl.ds(0, 512), pl.ds(512, 512)]

    def reduce_start(a):
        links.send(rs["ap"] + a, d.at[a, xo, :, :, ab[0]], x1a.at[a - 1], dev_xp)
        links.send(rs["bm"] + a, d.at[a, xo, :, :, ab[1]], x1b.at[a - 1], dev_xm)

    def reduce_merge(a):
        links.wait(rs["ap"] + a, x1a.at[a - 1], dev_xm)
        d[a, xp, :, :, ab[0]] = d[a, xp, :, :, ab[0]] + x1a[a - 1]
        links.send(rs["p"] + a, d.at[a, xp, po], x2a.at[a - 1, po], dev_xp)
        links.wait(rs["bm"] + a, x1b.at[a - 1], dev_xp)
        d[a, xm, :, :, ab[1]] = d[a, xm, :, :, ab[1]] + x1b[a - 1]
        links.send(rs["m"] + a, d.at[a, xm, po], x2b.at[a - 1, po], dev_xm)

    def reduce_own(a):
        links.send(rs["p2"] + a, d.at[a, xp, p], x2a.at[a - 1, p], dev_xp)
        links.send(rs["m2"] + a, d.at[a, xm, p], x2b.at[a - 1, p], dev_xm)

    def row_total(a, pp):
        return d[a, x, pp].astype(F32) + x2a[a - 1, pp].astype(F32) + x2b[a - 1, pp].astype(F32)

    def reduce_cross(a):
        links.wait(rs["p"] + a, x2a.at[a - 1, po], dev_xm)
        links.wait(rs["m"] + a, x2b.at[a - 1, po], dev_xp)
        es[a - 1] = row_total(a, po).astype(BF16)
        links.send(rs["y"] + a, es.at[a - 1], ry.at[a - 1], dev_yr)

    def reduce_finish(a):
        links.wait(rs["p2"] + a, x2a.at[a - 1, p], dev_xm)
        links.wait(rs["m2"] + a, x2b.at[a - 1, p], dev_xp)
        links.wait(rs["y"] + a, ry.at[a - 1], dev_yr)
        renew(a, row_total(a, p) + ry[a - 1].astype(F32))

    def renew(a, grad):
        unit = pl.ds(pl.multiple_of((2 * x + p) * 48, 16), 48)
        old = w[a, unit, :].astype(F32)
        norm = jnp.sqrt(jnp.sum(old * old, axis=1, keepdims=True) + EPS)
        stepped = old + RATE * norm / jnp.sqrt(jnp.sum(grad * grad, axis=1, keepdims=True) + EPS) * grad
        scale = norm / jnp.sqrt(jnp.sum(stepped * stepped, axis=1, keepdims=True) + EPS)
        new[a, x, p] = (stepped * scale).astype(BF16)

    direction(2, hid, val_all)
    reduce_start(2)
    backward(1 - yb)
    direction(1, grads.at[1], key_all)
    reduce_start(1)
    cross_ids = links.ids(5)

    def cross_ref(n, ref, lead):
        if n < 2:
            return ref.at[lead + (xo,) + ((po,) if lead else ()) + (slice(None), ab[n])]
        return ref.at[lead + ((xp, xm, x)[n - 2],) + ((po,) if lead else ())]

    def cross_send(n):
        links.send(cross_ids + n, cross_ref(n, d, (0,)), cross_ref(n, ry0, ()), dev_yr)

    def cross_add(n):
        links.wait(cross_ids + n, cross_ref(n, ry0, ()), dev_yr)
        if n < 2:
            d[0, xo, p, :, ab[n]] = d[0, xo, p, :, ab[n]] + ry0[xo, :, ab[n]]
        else:
            to_x = (xp, xm, x)[n - 2]
            d[0, to_x, p] = d[0, to_x, p] + ry0[to_x]

    direction(0, grads.at[0], key_all)
    cross_send(0)
    cross_send(1)
    reduce_merge(2)
    cross_send(2)
    cross_send(3)
    links.drain(40, 25)
    reduce_merge(1)
    cross_add(0)
    links.send(rs["ap"], d.at[0, xo, p, :, ab[0]], x1a0, dev_xp)
    cross_add(1)
    links.send(rs["bm"], d.at[0, xo, p, :, ab[1]], x1b0, dev_xm)
    reduce_own(2)
    reduce_cross(2)
    cross_send(4)
    links.drain(25, 25)
    cross_add(2)
    links.drain(25, 25)
    reduce_cross(1)
    links.wait(rs["ap"], x1a0, dev_xm)
    d[0, xp, p, :, ab[0]] = d[0, xp, p, :, ab[0]] + x1a0[...]
    links.send(rs["p"], d.at[0, xp, p], x2a0, dev_xp)
    cross_add(3)
    links.wait(rs["bm"], x1b0, dev_xp)
    d[0, xm, p, :, ab[1]] = d[0, xm, p, :, ab[1]] + x1b0[...]
    links.send(rs["m"], d.at[0, xm, p], x2b0, dev_xm)
    reduce_own(1)
    token_pass(2, "b")
    token_pass(2, "a")

    def n_piece(a, xx, other):
        return new.at[a, xx, po if other else p]

    def n_half(a, xx, other, h):
        return new.at[a, xx, po if other else p, :, ab[h]]

    n_start, n_start_y, n_cross, n_onward, n_far, n_finish = gather((0,), n_piece, n_half)
    links.drain(25, 25)
    reduce_finish(2)
    n_start(2)
    links.drain(25, 25)
    cross_add(4)
    links.wait(rs["p"], x2a0, dev_xm)
    links.wait(rs["m"], x2b0, dev_xp)
    renew(0, d[0, x, p].astype(F32) + x2a0[...].astype(F32) + x2b0[...].astype(F32))
    n_start(0)
    links.drain(25, 25)
    reduce_finish(1)
    n_start(1)
    token_pass(2, "c")
    links.drain(25, 25)
    n_onward(2)
    links.drain(25, 20)
    n_onward(0)
    n_cross(1)
    n_onward(1)
    n_cross(2)
    links.drain(25, 15)
    n_far(0)
    links.drain(25, 12)
    n_onward(1, 1)
    token_finish(2)

    core_ids = links.ids(4)
    y_ids = {(i, j): links.ids() for i in range(2) for j in range(4)}
    lo, hi = pl.ds(0, LOW), pl.ds(LOW, 384 - LOW)

    def queries(i):
        b = block(yb if i % 2 else 1 - yb, zlo if i < 2 else 1 - zlo)
        return qry_all[pl.ds(pl.multiple_of(b * 384, 16), 384), :]

    def gate(i):
        gate_next = dot(queries(i), new[0].reshape(384, 1024), NT)
        silu[i] = gate_next * jax.nn.sigmoid(gate_next)

    def activate(i):
        act[i] = (silu[i] * dot(queries(i), new[1].reshape(384, 1024), NT)).astype(BF16)

    def apply(i):
        term = dot(act[i], new[2].reshape(384, 1024), NN)
        for zz in range(4):
            for kk in range(2):
                at = (2 * zz + kk) * 128
                ob[i, kk, zz] = term[:, at:at + 128].astype(BF16)
        links.send(core_ids + i, ob.at[i, 1 - k], osib.at[i], dev_core)

    def both_cores(i):
        links.wait(core_ids + i, osib.at[i], dev_core)
        r[i // 2, i % 2] = ob[i, k] + osib[i]

    streams = ("far", "own", "y")
    ring = {(kind, sign): links.ids(4) for kind in streams for sign in (1, -1)}

    def to(step, sign):
        return ((z + sign * (4 - step) + 8) % 8) // 2

    targets = [(to(0, 1), to(2, 1), to(2, -1), zhi), (to(1, 1), to(1, -1), to(3, 1), to(3, -1))]

    def y_send(i, js):
        for j in js:
            t = targets[i][j]
            links.send(y_ids[i, j], r.at[i, 0, t, lo], ryo.at[i, t], dev_yt)

    def y_add(i, js):
        for j in js:
            t = targets[i][j]
            links.wait(y_ids[i, j], ryo.at[i, t], dev_yt)
            r[i, 1, t, lo] = r[i, 1, t, lo] + ryo[i, t]

    def chunk(kind, step, sign, part):
        base = 0 if kind == "y" else LOW
        return (step % 2, 0 if kind == "far" else 1, to(step, sign), pl.ds(base + part[0], part[1]))

    def span(kind, sign, step):
        size = LOW if kind == "y" else 384 - LOW
        if step:
            return 0, size
        return (0, size // 2) if sign > 0 else (size // 2, size // 2)


    def slot(kind, sign, step):
        n = 2 * streams.index(kind) + (0 if sign > 0 else 1)
        return slots.at[n, step, pl.ds(0, span(kind, sign, step)[1])]

    def ring_send(kind, sign, step):
        device = dev_zp if sign > 0 else dev_zm
        if kind == "far" and step == 3:
            device = dev_yt_zp if sign > 0 else dev_yt_zm
        links.send(ring[kind, sign] + step, r.at[chunk(kind, step, sign, span(kind, sign, step))],
                   slot(kind, sign, step), device)

    def ring_recv(kind, sign, step):
        got = slot(kind, sign, step)
        links.wait(ring[kind, sign] + step, got, dev_zm if sign > 0 else dev_zp)
        return got

    def ring_add(kind, sign, step):
        got = ring_recv(kind, sign, step)
        where = chunk(kind, step + 1, sign, span(kind, sign, step))
        r[where] = r[where] + got[...]

    def ring_step(kind, step):
        for sign in (1, -1):
            if step:
                ring_add(kind, sign, step - 1)
            ring_send(kind, sign, step)

    def ring_total(kind):
        got = [ring_recv(kind, sign, 3)[...].astype(F32) for sign in (1, -1)]
        return got[0] + got[1]

    n_finish(0)
    gate(0)
    gate(1)
    n_onward(2, 1)
    gate(2)
    gate(3)
    n_far(1)
    n_finish(1)
    for i in (0, 2, 1, 3):
        activate(i)
    n_far(2)
    n_finish(2)
    apply(0)
    apply(2)
    apply(1)
    both_cores(0)
    y_send(0, (0,))
    ring_step("far", 0)
    both_cores(2)
    y_send(1, (0, 1))
    y_send(0, (1, 2))
    apply(3)
    both_cores(1)
    ring_step("own", 0)
    links.drain(25, 12)
    y_add(0, (0,))
    ring_step("y", 0)
    y_send(1, (2, 3))
    y_send(0, (3,))
    fin_id = links.ids()
    links.send(fin_id, r.at[0, 0, zhi, hi], yfin, dev_yt)
    ring_step("far", 1)
    both_cores(3)
    links.drain(25, 12)
    y_add(1, (0, 1))
    ring_step("y", 1)
    ring_step("own", 1)
    ring_step("far", 2)
    y_add(0, (1, 2))
    links.drain(25, 12)
    ring_step("y", 2)
    ring_step("own", 2)
    ring_step("far", 3)
    y_add(1, (2, 3))
    links.drain(25, 10)
    ring_step("y", 3)
    ring_step("own", 3)
    y_add(0, (3,))
    links.drain(25, 6)
    links.wait(fin_id, yfin, dev_yt)
    fin[...] = r[0, 1, zhi, hi].astype(F32) + yfin[...].astype(F32) + ring_total("far")
    out_ref[hi, :] = (fin[...] + ring_total("own")).astype(BF16)
    out_ref[lo, :] = (r[0, 1, zhi, lo].astype(F32) + ring_total("y")).astype(BF16)
    links.drain()


def on_device(key_rows, value_rows, token_rates, query_rows, fast_gate, fast_up, fast_down):
    any_spec = pl.BlockSpec(memory_space=pl.ANY)
    vmem = pl.BlockSpec(memory_space=pltpu.VMEM)
    V = pltpu.VMEM
    scratch = [
        V((1536, 1024), BF16), V((1536, 1024), BF16), V((1536, 1024), BF16), V((1, 1536), F32),
        V((384,), F32), V((32, 3, 32, 384), BF16), V((3, 384, 1024), BF16),
        V((384, 1536), F32), V((384, 1536), F32), V((384, 1536), BF16), V((2, 384, 1536), BF16),
        V((3, 4, 2, 48, 1024), BF16),
        V((4, 48, 1024), BF16), V((48, 512), BF16), V((48, 512), BF16), V((48, 1024), BF16), V((48, 1024), BF16),
        V((2, 2, 48, 512), BF16), V((2, 2, 48, 512), BF16), V((2, 2, 48, 1024), BF16), V((2, 2, 48, 1024), BF16),
        V((2, 48, 1024), BF16), V((2, 48, 1024), BF16),
        V((3, 4, 2, 48, 1024), BF16),
        V((4, 384, 384), F32), V((4, 384, 384), BF16), V((4, 2, 4, 384, 128), BF16), V((4, 4, 384, 128), BF16), V((2, 2, 4, 384, 128), BF16),
        V((2, 4, LOW, 128), BF16), V((6, 4, max(LOW, 384 - LOW), 128), BF16),
        V((384 - LOW, 128), F32), V((384 - LOW, 128), BF16),
        pltpu.SemaphoreType.DMA((N_SEND,)), pltpu.SemaphoreType.DMA((N_RECV,)), pltpu.SemaphoreType.DMA((7,)),
    ]
    return pl.pallas_call(
        kernel,
        out_shape=pltpu.VMEM((384, 128), BF16),
        in_specs=[any_spec, any_spec, any_spec, any_spec, any_spec, any_spec, any_spec],
        out_specs=vmem,
        scratch_shapes=scratch,
        compiler_params=pltpu.CompilerParams(
            collective_id=0, has_side_effects=True, vmem_limit_bytes=58 * 2**20),
        name="ttt",
    )(key_rows, value_rows, token_rates, query_rows, fast_gate, fast_up, fast_down.T)


def solution(mesh):
    placed = (
        P("ctx", None), P("ctx", None), P("ctx"), P("ctx", None),
        P("ctx", "state"), P("ctx", "state"), P("state", "ctx"),
    )
    return jax.shard_map(
        on_device, mesh=mesh, in_specs=placed, out_specs=P("ctx", "state"), check_vma=False)
```

```python
import functools

import jax
import jax.numpy as jnp
from jax import lax
from jax.experimental import pallas as pl
from jax.experimental.pallas import tpu as pltpu
from jax.sharding import PartitionSpec as P

MESH = pl.DeviceIdType.MESH
EPS = 1e-06
RATE = 0.5
NT = (((1,), (1,)), ((), ()))
NN = (((1,), (0,)), ((), ()))
F32, BF16 = jnp.float32, jnp.bfloat16
N_SEND, N_RECV = 24, 145
LOW = 192


def dot(a, b, dims):
    return lax.dot_general(a, b, dims, preferred_element_type=F32)


def place(x, y, z, k):
    return (x * 8 + (z % 2) * 4 + y, (z // 2) * 2 + k)


class Links:
    def __init__(self, send_sem, recv_sem):
        self.send_sem, self.recv_sem, self.used, self.sent, self.turn = send_sem, recv_sem, 0, [], 0

    def ids(self, count=1):
        first = self.used
        self.used += count
        assert self.used <= N_RECV
        return first

    def copy(self, index, src, dst, device, turn=0):
        return pltpu.make_async_remote_copy(
            src_ref=src, dst_ref=dst, send_sem=self.send_sem.at[turn], recv_sem=self.recv_sem.at[index],
            device_id=device, device_id_type=MESH)

    def send(self, index, src, dst, device):
        if len(self.sent) == N_SEND:
            self.drain(1)
        copy = self.copy(index, src, dst, device, self.turn % N_SEND)
        self.turn += 1
        copy.start()
        self.sent.append(copy)

    def wait(self, index, dst, device):
        self.copy(index, dst, dst, device).wait_recv()

    def drain(self, most=300, keep=0):
        count = max(0, min(most, len(self.sent) - keep))
        for copy in self.sent[:count]:
            copy.wait_send()
        del self.sent[:count]


def kernel(key_ref, val_ref, rate_ref, qry_ref, gate_ref, up_ref, down_ref, out_ref,
           key_all, val_all, qry_all, rates, rate_row, raw, w, gp, uq, hid, grads,
           d, ry0, x1a0, x1b0, x2a0, x2b0, x1a, x1b, x2a, x2b, es, ry, new,
           silu, act, ob, osib, r, ryo, slots, fin, yfin,
           send_sem, recv_sem, local_sem):
    c, s = lax.axis_index("ctx"), lax.axis_index("state")
    x, zlo, y = c // 8, (c // 4) % 2, c % 4
    zhi, k = s // 2, s % 2
    z = 2 * zhi + zlo
    p, yb = y // 2, y % 2
    xp, xm, xo = (x + 1) % 4, (x + 3) % 4, (x + 2) % 4
    zp, zm = (z + 1) % 8, (z + 7) % 8
    yt = y + 1 - 2 * yb
    yr = 3 - y
    po = 1 - p
    y2 = ((y + 1) // 2) % 2
    links = Links(send_sem, recv_sem)
    z_pair = z + 1 - 2 * zlo
    dev_xp, dev_xm = place(xp, y, z, k), place(xm, y, z, k)
    dev_yt, dev_yr = place(x, yt, z, k), place(x, yr, z, k)
    dev_zp, dev_zm = place(x, y, zp, k), place(x, y, zm, k)
    dev_core = place(x, y, z, 1 - k)
    dev_pair, dev_diag = place(x, y, z_pair, k), place(x, yt, z_pair, k)
    dev_yt_zp, dev_yt_zm = place(x, yt, zp, k), place(x, yt, zm, k)

    barrier = pltpu.get_barrier_semaphore()
    for other in (dev_xp, dev_xm, dev_yt, dev_yr, dev_zp, dev_zm, dev_yt_zp, dev_yt_zm, dev_core):
        pl.semaphore_signal(barrier, inc=1, device_id=other, device_id_type=MESH)

    def block(yy, zz):
        return 2 * yy + zz

    me = block(yb, zlo)

    full = [key_all, val_all, qry_all]
    src = [key_ref, val_ref, qry_ref]
    weights = [gate_ref, up_ref, down_ref]

    def share(a, qz, q2):
        return weights[a].at[:, pl.ds(pl.multiple_of((qz * 2 + q2) * 384, 128), 384)]

    stay = []
    for a in range(3):
        copy = pltpu.make_async_copy(share(a, zlo, y2), raw.at[c, a], local_sem.at[a])
        copy.start()
        stay.append(copy)
    rate_copy = pltpu.make_async_copy(rate_ref, rate_row, local_sem.at[6])
    rate_copy.start()
    local = []
    for i in range(3):
        copy = pltpu.make_async_copy(
            src[i], full[i].at[pl.ds(pl.multiple_of(me * 384, 16), 384)], local_sem.at[3 + i])
        copy.start()
        local.append(copy)
    pl.semaphore_wait(barrier, 9)

    st = {j: links.ids() for j in (1, 2, 3)}
    for a in range(3):
        links.send(st[3], share(a, 1 - zlo, 1 - y2), raw.at[c, a], dev_diag)
        links.send(st[2], share(a, 1 - zlo, y2), raw.at[c, a], dev_pair)
    for a in range(3):
        links.send(st[1], share(a, zlo, 1 - y2), raw.at[c, a], dev_yt)

    blocks = {"a": block(1 - yb, zlo), "b": block(yb, 1 - zlo), "c": block(1 - yb, 1 - zlo)}
    fine = [[(0, 16), (16, 32), (96, 48), (48, 48), (144, 48)],
            [(0, 48), (96, 48), (48, 32), (144, 32), (80, 16), (176, 16)],
            [(0, 96), (96, 96)]]
    coarse = [(0, 96), (96, 96)]

    def parts(i, kind):
        return coarse if kind == "b" else fine[i]

    tok_ids = {(i, kind, h): links.ids() for i in range(3) for kind in "abc" for h in parts(i, kind)}
    sib_ids = {(i, kind): links.ids() for i in range(3) for kind in "abc"}

    def rows(i, b, h, kk=k):
        return full[i].at[pl.ds(pl.multiple_of(b * 384 + kk * 192 + h[0], 16), h[1])]

    z_to = [dev_zp, dev_zm]

    def a_start(i, h):
        mine = src[i].at[pl.ds(pl.multiple_of(k * 192 + h[0], 16), h[1])]
        links.send(tok_ids[i, "a", h], mine, rows(i, me, h), dev_yt)

    def b_start(i):
        for h in coarse:
            mine = src[i].at[pl.ds(pl.multiple_of(k * 192 + h[0], 16), h[1])]
            links.send(tok_ids[i, "b", h], mine, rows(i, me, h), z_to[h[0] // 96])

    def token_pass(i, kind, hs=None):
        for h in hs or parts(i, kind):
            here = rows(i, blocks[kind], h)
            links.wait(tok_ids[i, kind, h], here, dev_core)
            if kind == "a":
                links.send(tok_ids[i, "c", h], here, here, z_to[h[0] // 96])
            links.send(sib_ids[i, kind], here, here, dev_core)

    queue = [(i, h) for i in range(2) for h in fine[i]]

    def a_pass(n, ahead=3):
        i, h = queue[n]
        here = rows(i, blocks["a"], h)
        links.wait(tok_ids[i, "a", h], here, dev_core)
        if n + ahead < len(queue):
            a_start(*queue[n + ahead])
        links.send(tok_ids[i, "c", h], here, here, z_to[h[0] // 96])
        links.send(sib_ids[i, "a"], here, here, dev_core)

    def token_finish(i, kinds="abc"):
        for kind in kinds:
            links.wait(sib_ids[i, kind], rows(i, blocks[kind], (0, 192), 1 - k), dev_core)

    gather_ids = {}

    def gather(late, piece, half, turn=(0, 1, 2, 3)):
        ids = gather_ids

        def at(name, j):
            key = (name, turn[j])
            if key not in ids:
                ids[key] = links.ids()
            return ids[key]

        def move(name, j, ref, device):
            links.send(at(name, j), ref, ref, device)

        def start(j, along_y=True):
            if along_y:
                move("y", j, piece(j, x, 0), dev_yr)
            move("xp", j, piece(j, x, 0), dev_xp)
            move("xm", j, piece(j, x, 0), dev_xm)

        def start_y(j):
            move("y", j, piece(j, x, 0), dev_yr)

        def cross(j):
            links.wait(at("y", j), piece(j, x, 1), dev_yr)
            move("xp2", j, piece(j, x, 1), dev_xp)
            move("xm2", j, piece(j, x, 1), dev_xm)

        def onward(j, other=0):
            which = "2" if other else ""
            links.wait(at("xp" + which, j), piece(j, xm, other), dev_xm)
            move("fp" + which, j, half(j, xm, other, 0), dev_xp)
            if j in late:
                move("y1", j, piece(j, xm, 0), dev_yr)
            links.wait(at("xm" + which, j), piece(j, xp, other), dev_xp)
            move("fm" + which, j, half(j, xp, other, 1), dev_xm)
            if j in late:
                move("y2", j, piece(j, xp, 0), dev_yr)

        def far(j, other=0):
            which = "2" if other else ""
            links.wait(at("fp" + which, j), half(j, xo, other, 0), dev_xm)
            links.wait(at("fm" + which, j), half(j, xo, other, 1), dev_xp)
            if j in late:
                move("y3", j, piece(j, xo, 0), dev_yr)

        def finish(j):
            if j in late:
                links.wait(at("y", j), piece(j, x, 1), dev_yr)
                links.wait(at("y1", j), piece(j, xm, 1), dev_yr)
                links.wait(at("y2", j), piece(j, xp, 1), dev_yr)
                links.wait(at("y3", j), piece(j, xo, 1), dev_yr)
            else:
                far(j, 1)

        return start, start_y, cross, onward, far, finish

    def source(j, xx, other):
        yy = yt if j % 2 else y
        return xx * 8 + (1 - zlo if j >= 2 else zlo) * 4 + (3 - yy if other else yy)

    def w_piece(j, xx, other):
        return raw.at[source(j, xx, other)]

    def w_half(j, xx, other, h):
        return raw.at[source(j, xx, other), :, pl.ds(16 * h, 16)]

    w_start, w_start_y, w_cross, w_onward, w_far, w_finish = gather((2,), w_piece, w_half)
    for copy in stay:
        copy.wait()
    w_start(0)
    for n in range(3):
        a_start(*queue[n])
    b_start(0)
    rate_copy.wait()
    rate_id = links.ids(3)

    def rate_at(b):
        return rates.at[:, pl.ds(pl.multiple_of(b * 384, 128), 384)]

    rate_at(me)[...] = rate_row[...].reshape(1, 384)
    links.send(rate_id, rate_at(me), rate_at(me), dev_yt)
    links.send(rate_id + 1, rate_at(me), rate_at(me), dev_pair)
    links.send(rate_id + 2, rate_at(me), rate_at(me), dev_diag)

    def w_arrived(j):
        links.wait(st[j], raw.at[source(j, x, 0)], dev_core)
        w_start(j, j != 2)

    w_onward(0)
    w_cross(0)
    w_arrived(1)
    w_arrived(3)
    w_arrived(2)
    a_pass(0)
    w_onward(0, 1)
    a_pass(1)
    a_pass(2)
    w_cross(1)
    w_cross(3)
    w_start_y(2)
    a_pass(3)
    token_pass(0, "b")
    b_start(1)
    w_onward(2)
    w_onward(1)
    w_onward(3)
    a_pass(4)
    w_onward(1, 1)
    w_onward(3, 1)
    w_far(2)
    a_pass(5)
    a_pass(6)
    token_pass(0, "c", fine[0][:2])
    a_pass(7)
    token_pass(0, "c", fine[0][2:])
    token_pass(1, "b")
    for copy in local:
        copy.wait()
    for i, b in enumerate(("a", "b", "c")):
        links.wait(rate_id + i, rate_at(blocks[b]), dev_core)

    def upright(zz):
        for a in range(3):
            for xx in range(4):
                g = 2 * xx + zz
                w[a, :, pl.ds(pl.multiple_of(128 * g, 128), 128)] = (
                    raw[pl.ds(4 * g, 4), a].reshape(128, 384).astype(F32).T.astype(BF16))

    for j in (0, 1):
        w_far(j)
        w_finish(j)
    upright(zlo)
    w_far(3)
    w_finish(3)
    w_finish(2)
    a_pass(8)
    upright(1 - zlo)
    a_pass(9)
    a_pass(10)

    def forward(yy):
        cols = pl.ds(pl.multiple_of(yy * 768, 256), 768)
        keys = key_all[cols, :]
        gate_pre = dot(w[0], keys, NT)
        up_pre = dot(w[1], keys, NT)
        gp[:, cols] = gate_pre
        uq[:, cols] = up_pre
        hid[:, cols] = (gate_pre * jax.nn.sigmoid(gate_pre) * up_pre * rates[:, cols]).astype(BF16)

    def backward(yy):
        cols = pl.ds(pl.multiple_of(yy * 768, 256), 768)
        back = dot(w[2], val_all[cols, :], NT) * rates[:, cols]
        gate_pre, up_pre = gp[:, cols], uq[:, cols]
        sig = jax.nn.sigmoid(gate_pre)
        grads[0, :, cols] = (back * up_pre * sig * (1.0 + gate_pre * (1.0 - sig))).astype(BF16)
        grads[1, :, cols] = (back * gate_pre * sig).astype(BF16)

    token_finish(0, "b")
    forward(yb)
    token_pass(1, "c", fine[1][:3])
    token_finish(0, "ac")
    forward(1 - yb)
    token_pass(1, "c", fine[1][3:])
    token_finish(1, "b")
    backward(yb)
    token_finish(1, "ac")
    for h in fine[2]:
        a_start(2, h)
    b_start(2)

    def direction(a, acts, tokens):
        d[a] = dot(acts[...], tokens[...], NN).reshape(4, 2, 48, 1024).astype(BF16)

    rs = {name: links.ids(3) for name in ("ap", "bm", "p", "m", "p2", "m2", "y")}
    ab = [pl.ds(0, 512), pl.ds(512, 512)]

    def reduce_start(a):
        links.send(rs["ap"] + a, d.at[a, xo, :, :, ab[0]], x1a.at[a - 1], dev_xp)
        links.send(rs["bm"] + a, d.at[a, xo, :, :, ab[1]], x1b.at[a - 1], dev_xm)

    def reduce_merge(a):
        links.wait(rs["ap"] + a, x1a.at[a - 1], dev_xm)
        d[a, xp, :, :, ab[0]] = d[a, xp, :, :, ab[0]] + x1a[a - 1]
        links.send(rs["p"] + a, d.at[a, xp, po], x2a.at[a - 1, po], dev_xp)
        links.wait(rs["bm"] + a, x1b.at[a - 1], dev_xp)
        d[a, xm, :, :, ab[1]] = d[a, xm, :, :, ab[1]] + x1b[a - 1]
        links.send(rs["m"] + a, d.at[a, xm, po], x2b.at[a - 1, po], dev_xm)

    def reduce_own(a):
        links.send(rs["p2"] + a, d.at[a, xp, p], x2a.at[a - 1, p], dev_xp)
        links.send(rs["m2"] + a, d.at[a, xm, p], x2b.at[a - 1, p], dev_xm)

    def row_total(a, pp):
        return d[a, x, pp].astype(F32) + x2a[a - 1, pp].astype(F32) + x2b[a - 1, pp].astype(F32)

    def reduce_cross(a):
        links.wait(rs["p"] + a, x2a.at[a - 1, po], dev_xm)
        links.wait(rs["m"] + a, x2b.at[a - 1, po], dev_xp)
        es[a - 1] = row_total(a, po).astype(BF16)
        links.send(rs["y"] + a, es.at[a - 1], ry.at[a - 1], dev_yr)

    def reduce_finish(a):
        links.wait(rs["p2"] + a, x2a.at[a - 1, p], dev_xm)
        links.wait(rs["m2"] + a, x2b.at[a - 1, p], dev_xp)
        links.wait(rs["y"] + a, ry.at[a - 1], dev_yr)
        renew(a, row_total(a, p) + ry[a - 1].astype(F32))

    def renew(a, grad):
        unit = pl.ds(pl.multiple_of((2 * x + p) * 48, 16), 48)
        old = w[a, unit, :].astype(F32)
        norm = jnp.sqrt(jnp.sum(old * old, axis=1, keepdims=True) + EPS)
        stepped = old + RATE * norm / jnp.sqrt(jnp.sum(grad * grad, axis=1, keepdims=True) + EPS) * grad
        scale = norm / jnp.sqrt(jnp.sum(stepped * stepped, axis=1, keepdims=True) + EPS)
        new[a, x, p] = (stepped * scale).astype(BF16)

    direction(2, hid, val_all)
    reduce_start(2)
    backward(1 - yb)
    direction(1, grads.at[1], key_all)
    reduce_start(1)
    cross_ids = links.ids(5)

    def cross_ref(n, ref, lead):
        if n < 2:
            return ref.at[lead + (xo,) + ((po,) if lead else ()) + (slice(None), ab[n])]
        return ref.at[lead + ((xp, xm, x)[n - 2],) + ((po,) if lead else ())]

    def cross_send(n):
        links.send(cross_ids + n, cross_ref(n, d, (0,)), cross_ref(n, ry0, ()), dev_yr)

    def cross_add(n):
        links.wait(cross_ids + n, cross_ref(n, ry0, ()), dev_yr)
        if n < 2:
            d[0, xo, p, :, ab[n]] = d[0, xo, p, :, ab[n]] + ry0[xo, :, ab[n]]
        else:
            to_x = (xp, xm, x)[n - 2]
            d[0, to_x, p] = d[0, to_x, p] + ry0[to_x]

    direction(0, grads.at[0], key_all)
    cross_send(0)
    cross_send(1)
    reduce_merge(2)
    cross_send(2)
    cross_send(3)
    links.drain(40, 25)
    reduce_merge(1)
    cross_add(0)
    links.send(rs["ap"], d.at[0, xo, p, :, ab[0]], x1a0, dev_xp)
    cross_add(1)
    links.send(rs["bm"], d.at[0, xo, p, :, ab[1]], x1b0, dev_xm)
    reduce_own(2)
    reduce_cross(2)
    cross_send(4)
    links.drain(25, 25)
    cross_add(2)
    links.drain(25, 25)
    reduce_cross(1)
    links.wait(rs["ap"], x1a0, dev_xm)
    d[0, xp, p, :, ab[0]] = d[0, xp, p, :, ab[0]] + x1a0[...]
    links.send(rs["p"], d.at[0, xp, p], x2a0, dev_xp)
    cross_add(3)
    links.wait(rs["bm"], x1b0, dev_xp)
    d[0, xm, p, :, ab[1]] = d[0, xm, p, :, ab[1]] + x1b0[...]
    links.send(rs["m"], d.at[0, xm, p], x2b0, dev_xm)
    reduce_own(1)
    token_pass(2, "b")
    token_pass(2, "a")

    def n_piece(a, xx, other):
        return new.at[a, xx, po if other else p]

    def n_half(a, xx, other, h):
        return new.at[a, xx, po if other else p, :, ab[h]]

    n_start, n_start_y, n_cross, n_onward, n_far, n_finish = gather((0,), n_piece, n_half, (2, 0, 1))
    links.drain(25, 25)
    reduce_finish(2)
    n_start(2)
    links.drain(25, 25)
    cross_add(4)
    links.wait(rs["p"], x2a0, dev_xm)
    links.wait(rs["m"], x2b0, dev_xp)
    renew(0, d[0, x, p].astype(F32) + x2a0[...].astype(F32) + x2b0[...].astype(F32))
    n_start(0)
    links.drain(25, 25)
    reduce_finish(1)
    n_start(1)
    token_pass(2, "c")
    links.drain(25, 25)
    n_onward(2)
    links.drain(25, 20)
    n_onward(0)
    n_cross(1)
    n_onward(1)
    n_cross(2)
    links.drain(25, 15)
    n_far(0)
    links.drain(25, 12)
    n_onward(1, 1)
    token_finish(2)

    core_ids = links.ids(4)
    y_ids = {(i, j): links.ids() for i in range(2) for j in range(4)}
    lo, hi = pl.ds(0, LOW), pl.ds(LOW, 384 - LOW)

    def queries(i):
        b = block(yb if i % 2 else 1 - yb, zlo if i < 2 else 1 - zlo)
        return qry_all[pl.ds(pl.multiple_of(b * 384, 16), 384), :]

    def gate(i):
        gate_next = dot(queries(i), new[0].reshape(384, 1024), NT)
        silu[i] = gate_next * jax.nn.sigmoid(gate_next)

    def activate(i):
        act[i] = (silu[i] * dot(queries(i), new[1].reshape(384, 1024), NT)).astype(BF16)

    def apply(i):
        term = dot(act[i], new[2].reshape(384, 1024), NN)
        for zz in range(4):
            for kk in range(2):
                at = (2 * zz + kk) * 128
                ob[i, kk, zz] = term[:, at:at + 128].astype(BF16)
        links.send(core_ids + i, ob.at[i, 1 - k], osib.at[i], dev_core)

    def both_cores(i):
        links.wait(core_ids + i, osib.at[i], dev_core)
        r[i // 2, i % 2] = ob[i, k] + osib[i]

    streams = ("far", "own", "y")
    ring = {(kind, sign): links.ids(4) for kind in streams for sign in (1, -1)}

    def to(step, sign):
        return ((z + sign * (4 - step) + 8) % 8) // 2

    targets = [(to(0, 1), to(2, 1), to(2, -1), zhi), (to(1, 1), to(1, -1), to(3, 1), to(3, -1))]

    def y_send(i, js):
        for j in js:
            t = targets[i][j]
            links.send(y_ids[i, j], r.at[i, 0, t, lo], ryo.at[i, t], dev_yt)

    def y_add(i, js):
        for j in js:
            t = targets[i][j]
            links.wait(y_ids[i, j], ryo.at[i, t], dev_yt)
            r[i, 1, t, lo] = r[i, 1, t, lo] + ryo[i, t]

    def chunk(kind, step, sign, part):
        base = 0 if kind == "y" else LOW
        return (step % 2, 0 if kind == "far" else 1, to(step, sign), pl.ds(base + part[0], part[1]))

    def span(kind, sign, step):
        size = LOW if kind == "y" else 384 - LOW
        if step:
            return 0, size
        return (0, size // 2) if sign > 0 else (size // 2, size // 2)


    def slot(kind, sign, step):
        n = 2 * streams.index(kind) + (0 if sign > 0 else 1)
        return slots.at[n, step, pl.ds(0, span(kind, sign, step)[1])]

    def ring_send(kind, sign, step):
        device = dev_zp if sign > 0 else dev_zm
        if kind == "far" and step == 3:
            device = dev_yt_zp if sign > 0 else dev_yt_zm
        links.send(ring[kind, sign] + step, r.at[chunk(kind, step, sign, span(kind, sign, step))],
                   slot(kind, sign, step), device)

    def ring_recv(kind, sign, step):
        got = slot(kind, sign, step)
        links.wait(ring[kind, sign] + step, got, dev_zm if sign > 0 else dev_zp)
        return got

    def ring_add(kind, sign, step):
        got = ring_recv(kind, sign, step)
        where = chunk(kind, step + 1, sign, span(kind, sign, step))
        r[where] = r[where] + got[...]

    def ring_step(kind, step):
        for sign in (1, -1):
            if step:
                ring_add(kind, sign, step - 1)
            ring_send(kind, sign, step)

    def ring_total(kind):
        got = [ring_recv(kind, sign, 3)[...].astype(F32) for sign in (1, -1)]
        return got[0] + got[1]

    n_finish(0)
    gate(0)
    gate(1)
    n_onward(2, 1)
    gate(2)
    gate(3)
    n_far(1)
    n_finish(1)
    for i in (0, 2, 1, 3):
        activate(i)
    n_far(2)
    n_finish(2)
    apply(0)
    apply(2)
    apply(1)
    both_cores(0)
    y_send(0, (0,))
    ring_step("far", 0)
    both_cores(2)
    y_send(1, (0, 1))
    y_send(0, (1, 2))
    apply(3)
    both_cores(1)
    ring_step("own", 0)
    links.drain(25, 12)
    y_add(0, (0,))
    ring_step("y", 0)
    y_send(1, (2, 3))
    y_send(0, (3,))
    fin_id = links.ids()
    links.send(fin_id, r.at[0, 0, zhi, hi], yfin, dev_yt)
    ring_step("far", 1)
    both_cores(3)
    links.drain(25, 12)
    y_add(1, (0, 1))
    ring_step("y", 1)
    ring_step("own", 1)
    ring_step("far", 2)
    y_add(0, (1, 2))
    links.drain(25, 12)
    ring_step("y", 2)
    ring_step("own", 2)
    ring_step("far", 3)
    y_add(1, (2, 3))
    links.drain(25, 10)
    ring_step("y", 3)
    ring_step("own", 3)
    y_add(0, (3,))
    links.drain(25, 6)
    links.wait(fin_id, yfin, dev_yt)
    fin[...] = r[0, 1, zhi, hi].astype(F32) + yfin[...].astype(F32) + ring_total("far")
    out_ref[hi, :] = (fin[...] + ring_total("own")).astype(BF16)
    out_ref[lo, :] = (r[0, 1, zhi, lo].astype(F32) + ring_total("y")).astype(BF16)
    links.drain()


def on_device(key_rows, value_rows, token_rates, query_rows, fast_gate, fast_up, fast_down):
    any_spec = pl.BlockSpec(memory_space=pl.ANY)
    vmem = pl.BlockSpec(memory_space=pltpu.VMEM)
    V = pltpu.VMEM
    scratch = [
        V((1536, 1024), BF16), V((1536, 1024), BF16), V((1536, 1024), BF16), V((1, 1536), F32),
        V((384,), F32), V((32, 3, 32, 384), BF16), V((3, 384, 1024), BF16),
        V((384, 1536), F32), V((384, 1536), F32), V((384, 1536), BF16), V((2, 384, 1536), BF16),
        V((3, 4, 2, 48, 1024), BF16),
        V((4, 48, 1024), BF16), V((48, 512), BF16), V((48, 512), BF16), V((48, 1024), BF16), V((48, 1024), BF16),
        V((2, 2, 48, 512), BF16), V((2, 2, 48, 512), BF16), V((2, 2, 48, 1024), BF16), V((2, 2, 48, 1024), BF16),
        V((2, 48, 1024), BF16), V((2, 48, 1024), BF16),
        V((3, 4, 2, 48, 1024), BF16),
        V((4, 384, 384), F32), V((4, 384, 384), BF16), V((4, 2, 4, 384, 128), BF16), V((4, 4, 384, 128), BF16), V((2, 2, 4, 384, 128), BF16),
        V((2, 4, LOW, 128), BF16), V((6, 4, max(LOW, 384 - LOW), 128), BF16),
        V((384 - LOW, 128), F32), V((384 - LOW, 128), BF16),
        pltpu.SemaphoreType.DMA((N_SEND,)), pltpu.SemaphoreType.DMA((N_RECV,)), pltpu.SemaphoreType.DMA((7,)),
    ]
    return pl.pallas_call(
        kernel,
        out_shape=pltpu.VMEM((384, 128), BF16),
        in_specs=[any_spec, any_spec, any_spec, any_spec, any_spec, any_spec, any_spec],
        out_specs=vmem,
        scratch_shapes=scratch,
        compiler_params=pltpu.CompilerParams(
            collective_id=0, has_side_effects=True, vmem_limit_bytes=58 * 2**20),
        name="ttt",
    )(key_rows, value_rows, token_rates, query_rows, fast_gate, fast_up, fast_down.T)


def solution(mesh):
    placed = (
        P("ctx", None), P("ctx", None), P("ctx"), P("ctx", None),
        P("ctx", "state"), P("ctx", "state"), P("state", "ctx"),
    )
    return jax.shard_map(
        on_device, mesh=mesh, in_specs=placed, out_specs=P("ctx", "state"), check_vma=False)
```
